512 devices in a mesh: gx: 16 (over y, core), gy: 32 (over z, x).
Axes of the slice: x: 4, y: 8, z: 8, core: 2. Of those that a mesh axis runs over, the one named last changes fastest.
Arguments:
- misfit: float32 [384, 768, 128], P('gx', 'gy'), may hold values from -6 to 6
- bleach_mask: int32 [384, 768, 128], P('gx', 'gy'), may hold values 0 or 1
- labels: int32 [384, 768, 128], P('gx', 'gy'), may hold values from 0 to 2
- diffusion: float32 [384, 768, 128], P('gx', 'gy'), may hold values from 0.01 to 0.08
- bind_table: float32 [3], replicated, may hold values from 0.05 to 0.4
- release_table: float32 [3], replicated, may hold values from 0.05 to 0.4
- kern_x: float32 [31], replicated, may hold values from 0.1 to 0.3
- kern_y: float32 [31], replicated, may hold values from 0.1 to 0.3
- kern_z: float32 [63], replicated, may hold values from 0.05 to 0.2
- free_states: bfloat16 [2, 384, 768, 128], P(None, 'gx', 'gy'), may hold values from 0 to 2
Outputs:
- diff_grad: float32 [384, 768, 128], P('gx', 'gy')
- adjoint_initial: float32 [2, 384, 768, 128], P(None, 'gx', 'gy')
The draws below stay inside these ranges and needn't reach their ends.
All inputs are finite; a program needn't handle non-finite values. No bound on the sum of `bleach_mask` on one device may be relied on, other than what follows from the above.
Results may differ from the reference program's by a relative error of at most 0.0003.
Values may be sent and summed in bfloat16 or wider, within the bound.
No kernel may reach another device: no remote copies, remote signals or barrier semaphores. Data moves between devices by JAX's collectives and lax.ppermute only.
A program may use at most 64 MiB of HBM per device.

```python
import math
import jax
import jax.numpy as jnp
from jax import lax

NZ = 128
REACH = 15
REACH_Z = 31
STEPS = 2
NCOMP = 3
NX = 384
NY = 768


def place_ends(drawn, stream_key, low, top_value):
    longest = drawn.shape.index(max(drawn.shape))
    spots = []
    for shift in (0, 1):
        where = [jax.random.randint(jax.random.fold_in(stream_key, axis), (), 0, length) for axis, length in enumerate(drawn.shape)]
        where[longest] = (where[longest] + shift) % drawn.shape[longest]
        spots.append(tuple(where))
    return drawn.at[spots[0]].set(low).at[spots[1]].set(top_value)


def level_of(rng, extent, cuts, smallest, high):
    factor_of = 1.0
    for axis_at, parts in cuts:
        heights = jax.random.uniform(jax.random.fold_in(jax.random.fold_in(rng, 6), axis_at), (parts,), jnp.float32, smallest / len(cuts), high / len(cuts))
        factor_of = factor_of * jnp.repeat(jnp.exp(heights), extent[axis_at] // parts).reshape((-1,) + (1,) * (len(extent) - 1 - axis_at))
    return factor_of


def normal_values(key, dims, scale, bound, pieces=(), held_as=jnp.bfloat16):
    array = jax.random.normal(key, dims, jnp.float32) * scale
    if len(pieces) > 0:
        array = level_of(key, dims, pieces, -0.22, 0.18) * array
    return jnp.clip(array, min=-bound, max=bound).astype(held_as)


def setup_inputs(seed: int = 0) -> dict:
    streams_of = jax.random.split(jax.random.key(seed), 11)
    return {
        "misfit": normal_values(streams_of[0], (NX, NY, NZ), 1.0, 6.0, ((0, 16), (1, 32)), jnp.float32),
        "bleach_mask": place_ends((jax.random.randint(streams_of[1], (NX, NY, NZ), 0, 4) < 1).astype(jnp.int32), jax.random.fold_in(streams_of[1], 1), 0, 1),
        "labels": place_ends(jax.random.randint(streams_of[2], (NX, NY, NZ), 0, NCOMP), jax.random.fold_in(streams_of[2], 1), 0, NCOMP - 1).astype(jnp.int32),
        "diffusion": jnp.clip(jnp.exp(math.log(0.08) - 2.0794415 * jax.random.uniform(streams_of[3], (NX, NY, NZ), jnp.float32) ** level_of(streams_of[3], (NX, NY, NZ), ((0, 16), (1, 32)), -0.2, 0.2)), 0.01, 0.08),
        "bind_table": jnp.clip(jnp.exp(jax.random.uniform(streams_of[4], (NCOMP,), jnp.float32, math.log(0.05), math.log(0.4))), 0.05, 0.4),
        "release_table": jnp.clip(jnp.exp(jax.random.uniform(streams_of[5], (NCOMP,), jnp.float32, math.log(0.05), math.log(0.4))), 0.05, 0.4),
        "kern_x": jnp.clip(jax.random.uniform(streams_of[6], (2 * REACH + 1,), jnp.float32, 0.1, 0.3), 0.1, 0.3),
        "kern_y": jnp.clip(jax.random.uniform(streams_of[7], (2 * REACH + 1,), jnp.float32, 0.1, 0.3), 0.1, 0.3),
        "kern_z": jnp.clip(jax.random.uniform(streams_of[8], (2 * REACH_Z + 1,), jnp.float32, 0.05, 0.2), 0.05, 0.2),
        "free_states": jnp.clip(2.0 * jax.random.uniform(streams_of[9], (STEPS, NX, NY, NZ), jnp.float32) ** level_of(streams_of[9], (STEPS, NX, NY, NZ), ((1, 16), (2, 32)), -0.2, 0.2), 0.0, 2.0).astype(jnp.bfloat16),
    }


def band_matrix(kern, size, blur_reach):
    row_index = jnp.arange(size, dtype=jnp.int32)[:, None]
    col_index = jnp.arange(size, dtype=jnp.int32)[None, :]
    offset = col_index - row_index + blur_reach
    valid = (offset >= 0) & (offset <= 2 * blur_reach)
    picked = jnp.take(kern, jnp.clip(offset, 0, 2 * blur_reach))
    return jnp.where(valid, picked, jnp.zeros_like(picked))


def face_slices(padded):
    return [padded[2:, 1:-1, 1:-1], padded[:-2, 1:-1, 1:-1],
            padded[1:-1, 2:, 1:-1], padded[1:-1, :-2, 1:-1],
            padded[1:-1, 1:-1, 2:], padded[1:-1, 1:-1, :-2]]


def reference(misfit, bleach_mask, labels, diffusion, bind_table, release_table, kern_x, kern_y, kern_z, free_states):
    highest = lax.Precision.HIGHEST
    weighted = (1.0 + 3.0 * bleach_mask.astype(jnp.float32)) * misfit
    zmatrix = band_matrix(kern_z, NZ, REACH_Z)
    xmatrix = band_matrix(kern_x, NX, REACH)
    ymatrix = band_matrix(kern_y, NY, REACH)
    partial_blur = jnp.einsum('xyz,wz->xyw', weighted, zmatrix, precision=highest)
    partial_blur = jnp.einsum('vx,xyz->vyz', xmatrix, partial_blur, precision=highest)
    image_adjoint = jnp.einsum('wy,xyz->xwz', ymatrix, partial_blur, precision=highest)
    bind = jnp.zeros_like(diffusion)
    release = jnp.zeros_like(diffusion)
    for kind in range(NCOMP):
        hit = labels == kind
        bind = jnp.where(hit, bind_table[kind], bind)
        release = jnp.where(hit, release_table[kind], release)
    coeff_near = face_slices(jnp.pad(diffusion, 1))
    adj_free = image_adjoint
    adj_bound = 0.5 * image_adjoint
    diff_grad = jnp.zeros_like(diffusion)
    for step in reversed(range(STEPS)):
        state = free_states[step].astype(jnp.float32)
        state_near = face_slices(jnp.pad(state, 1))
        adj_near = face_slices(jnp.pad(adj_free, 1))
        spread = jnp.zeros_like(diffusion)
        for other, state_other, adj_other in zip(coeff_near, state_near, adj_near):
            total = diffusion + other
            coupling = 2.0 * diffusion * other / total
            slope = 2.0 * other * other / (total * total)
            change = adj_other - adj_free
            spread = spread + coupling * change
            diff_grad = diff_grad - slope * (state_other - state) * change
        new_free = adj_free + spread - bind * adj_free + bind * adj_bound
        adj_bound = adj_bound + release * adj_free - release * adj_bound
        adj_free = new_free
    return diff_grad, jnp.stack([adj_free, adj_bound])
```

```python
import functools

import jax
import jax.numpy as jnp
from jax import lax
from jax.experimental import pallas as pl
from jax.experimental.pallas import tpu as pltpu
from jax.sharding import PartitionSpec as P

AXES = ("gx", "gy")
RIM = 2
JOFF = 4
SLOT = 32


def blur(read, write, taps, count, span, group):
    for start in range(0, count, group):
        outs = range(start, min(start + group, count))
        acc = {}
        for e in range(outs[0], outs[-1] + span):
            value = read(e)
            for i in outs:
                if 0 <= e - i < span:
                    term = taps[e - i] * value
                    acc[i] = acc[i] + term if i in acc else term
            if e - (span - 1) in acc:
                i = e - (span - 1)
                write(i, acc.pop(i))


def first_kernel(reach, misfit, mask, labels, diffusion, states, kern_z, own, one, two, zrow, work, edge):
    rows_x = states.shape[1]
    depth = misfit.shape[1]
    nx, ny = rows_x, misfit.shape[0] // rows_x
    taps_z = kern_z.shape[1]
    half = (taps_z - 1) // 2
    zrow[...] = jnp.zeros_like(zrow)
    zrow[0:1, 0:taps_z] = kern_z[...]
    spread = jnp.broadcast_to(zrow[0:1, :], (depth, depth))
    rolled = pltpu.roll(spread, depth - half, 1, stride=1, stride_axis=0)
    w = lax.broadcasted_iota(jnp.int32, (depth, depth), 0)
    z = lax.broadcasted_iota(jnp.int32, (depth, depth), 1)
    matrix = jnp.where(jnp.abs(z - w) <= half, rolled, 0.0)
    weighted = (1.0 + 3.0 * mask[...].astype(jnp.float32)) * misfit[...]
    work[...] = lax.dot_general(
        weighted, matrix, (((1,), (1,)), ((), ())),
        precision=lax.Precision.HIGHEST, preferred_element_type=jnp.float32)
    edge[...] = states[...].astype(jnp.float32).reshape(edge.shape)
    octets = nx // 8
    for y in range(ny):
        for o in range(octets):
            own[y, pl.ds(8 * o, 8), :] = work[pl.ds(8 * o * ny + y, 8, stride=ny), :]
    right_first = (lax.axis_index("gx") + lax.axis_index("gy")) % 2 == 0
    width = reach + RIM

    def pack(out, right):
        start = ny - width if right else 0
        for y in range(width):
            out[y] = own[start + y]
        for k in range(RIM):
            y = ny - RIM + k if right else k
            for o in range(octets):
                out[width + k, pl.ds(8 * o, 8), :] = diffusion[pl.ds(8 * o * ny + y, 8, stride=ny), :]
        y = ny - 1 if right else 0
        for o in range(octets):
            here = pl.ds(8 * o * ny + y, 8, stride=ny)
            out[width + RIM, pl.ds(8 * o, 8), :] = labels[here, :].astype(jnp.float32)
            for s in range(states.shape[0]):
                at = pl.ds((s * nx + 8 * o) * ny + y, 8, stride=ny)
                out[width + RIM + 1 + s, pl.ds(8 * o, 8), :] = edge[at, :]

    @pl.when(right_first)
    def _():
        pack(one, True)
        pack(two, False)

    @pl.when(jnp.logical_not(right_first))
    def _():
        pack(one, False)
        pack(two, True)


def second_kernel(own, one, two, labels, diffusion, states, kern_y, blurred, outer, inner, ext, side):
    ny, nx, depth = own.shape
    span = kern_y.shape[0]
    reach = (span - 1) // 2
    width = reach + RIM
    tall = ny + 2 * RIM
    octets = nx // 8
    right_first = (lax.axis_index("gx") + lax.axis_index("gy")) % 2 == 0

    def place(left, right):
        for y in range(width):
            ext[y] = left[y]
            ext[width + ny + y] = right[y]
        for k in range(left.shape[0] - width):
            side[0, k] = left[width + k]
            side[1, k] = right[width + k]

    @pl.when(right_first)
    def _():
        place(two, one)

    @pl.when(jnp.logical_not(right_first))
    def _():
        place(one, two)

    ext[pl.ds(width, ny)] = own[...]
    taps = [kern_y[t] for t in range(span)]
    for o in range(octets):
        def read(e):
            return ext[e, pl.ds(8 * o, 8), :]

        def write(j, value):
            blurred[pl.ds(8 * o * SLOT + JOFF - RIM + j, 8, stride=SLOT), :] = value

        blur(read, write, taps, tall, span, 14)

    def pack(out, upper):
        at = 0
        first = nx - width if upper else 0
        for x in range(first, first + width):
            out[pl.ds(at, tall), :] = blurred[pl.ds(x * SLOT + JOFF - RIM, tall), :]
            at += tall
        for k in range(RIM):
            x = nx - RIM + k if upper else k
            for r in range(RIM):
                out[pl.ds(at + r, 1), :] = side[0, r, pl.ds(x, 1), :]
                out[pl.ds(at + RIM + ny + r, 1), :] = side[1, r, pl.ds(x, 1), :]
            out[pl.ds(at + RIM, ny), :] = diffusion[x]
            at += tall
        x = nx - 1 if upper else 0
        out[pl.ds(at, ny), :] = labels[x].astype(jnp.float32)
        at += ny
        for s in range(states.shape[0]):
            out[pl.ds(at, ny), :] = states[s, x].astype(jnp.float32)
            at += ny

    even = lax.axis_index("gx") % 2 == 0

    @pl.when(even)
    def _():
        pack(inner, True)
        pack(outer, False)

    @pl.when(jnp.logical_not(even))
    def _():
        pack(inner, False)
        pack(outer, True)


def third_kernel(blurred, outer, inner, one, two, labels, diffusion, states, kern_x, bind_t, release_t,
                 grad, adjoint, ext, image, adj, coef, state, kind):
    nx, ny, depth = labels.shape
    steps = states.shape[0]
    span = kern_x.shape[0]
    reach = (span - 1) // 2
    width = reach + RIM
    tall = ny + 2 * RIM
    octets = nx // 8
    high = image.shape[1]
    right_first = (lax.axis_index("gx") + lax.axis_index("gy")) % 2 == 0
    even = lax.axis_index("gx") % 2 == 0
    lo, n_in = JOFF - RIM, slice(JOFF, JOFF + ny)

    def place(slab, upper):
        at = 0
        base = width + nx if upper else 0
        for k in range(width):
            ext[base + k, lo:lo + tall, :] = slab[pl.ds(at, tall), :]
            at += tall
        order = range(nx + RIM, nx + 2 * RIM) if upper else range(RIM)
        for i in order:
            coef[i, lo:lo + tall, :] = slab[pl.ds(at, tall), :]
            at += tall
        i = nx + 1 if upper else 0
        kind[i, n_in, :] = slab[pl.ds(at, ny), :]
        at += ny
        for s in range(steps):
            state[s, i, n_in, :] = slab[pl.ds(at, ny), :]
            at += ny

    @pl.when(even)
    def _():
        place(outer, False)
        place(inner.at[1], True)

    @pl.when(jnp.logical_not(even))
    def _():
        place(inner.at[0], False)
        place(outer, True)

    for x in range(nx):
        ext[width + x, 0:SLOT, :] = blurred[pl.ds(x * SLOT, SLOT), :]
        coef[RIM + x, n_in, :] = diffusion[x]
        kind[1 + x, n_in, :] = labels[x].astype(jnp.float32)
        for s in range(steps):
            state[s, 1 + x, n_in, :] = states[s, x].astype(jnp.float32)

    def rims(left, right):
        for x in range(nx):
            row = pl.ds(x, 1)
            for k in range(RIM):
                coef[RIM + x, JOFF - RIM + k:JOFF - RIM + k + 1, :] = left[width + k, row, :]
                coef[RIM + x, JOFF + ny + k:JOFF + ny + k + 1, :] = right[width + k, row, :]
            kind[1 + x, JOFF - 1:JOFF, :] = left[width + RIM, row, :]
            kind[1 + x, JOFF + ny:JOFF + ny + 1, :] = right[width + RIM, row, :]
            for s in range(steps):
                state[s, 1 + x, JOFF - 1:JOFF, :] = left[width + RIM + 1 + s, row, :]
                state[s, 1 + x, JOFF + ny:JOFF + ny + 1, :] = right[width + RIM + 1 + s, row, :]

    @pl.when(right_first)
    def _():
        rims(two, one)

    @pl.when(jnp.logical_not(right_first))
    def _():
        rims(one, two)

    taps = [kern_x[t] for t in range(span)]

    @pl.loop(0, SLOT // 8)
    def _(v):
        rows = pl.ds(pl.multiple_of(8 * v, 8), 8)

        def write(i, value):
            image[i, rows, :] = value

        blur(lambda e: ext[e, rows, :], write, taps, nx + 2 * RIM, span, 14)

    def rate(code, table):
        return jnp.where(code == 0, table[0], jnp.where(code == 1, table[1], table[2]))

    def inside(rows):
        return lax.broadcasted_iota(jnp.int32, (rows, depth), 1) < depth - 1

    def ratio(here, there):
        inverse = 1.0 / jnp.maximum(here + there, 1e-30)
        return there * inverse, here * inverse

    @pl.loop(0, nx + 2)
    def _(i):
        h = slice(JOFF - 2, JOFF - 2 + SLOT)
        a, d = image[i + 1, h, :], coef[i + 1, h, :]

        def flux(a_there, d_there):
            q, _ = ratio(d, d_there)
            return 2.0 * d * q * (a_there - a)

        last = inside(SLOT)
        up = JOFF - 1
        total = flux(image[i + 2, h, :], coef[i + 2, h, :]) + flux(image[i, h, :], coef[i, h, :])
        total += flux(image[i + 1, up:up + SLOT, :], coef[i + 1, up:up + SLOT, :])
        total += flux(image[i + 1, up - 2:up - 2 + SLOT, :], coef[i + 1, up - 2:up - 2 + SLOT, :])
        fz = jnp.where(last, flux(pltpu.roll(a, depth - 1, 1), pltpu.roll(d, depth - 1, 1)), 0.0)
        total += fz - pltpu.roll(fz, 1, 1)
        bind = rate(kind[i, h, :], bind_t)
        adj[i, h, :] = a + total - 0.5 * bind * a

    @pl.loop(0, nx)
    def _(x):
        i = x + 1
        h = n_in
        d, a1, a0 = coef[i + 1, h, :], image[i + 1, h, :], adj[i, h, :]
        s1, s0 = state[steps - 1, i, h, :], state[0, i, h, :]

        def face(di, shift):
            g = slice(JOFF + shift, JOFF + shift + ny)
            q, _ = ratio(d, coef[i + 1 + di, g, :])
            change1 = image[i + 1 + di, g, :] - a1
            change0 = adj[i + di, g, :] - a0
            both = (state[steps - 1, i + di, g, :] - s1) * change1 + (state[0, i + di, g, :] - s0) * change0
            return d * q * change0, q * q * both

        total, slopes = face(1, 0)
        for di, shift in ((-1, 0), (0, 1), (0, -1)):
            f, p = face(di, shift)
            total, slopes = total + f, slopes + p
        last = inside(ny)
        nxt = functools.partial(pltpu.roll, shift=depth - 1, axis=1)
        q, p = ratio(d, nxt(d))
        change1, change0 = nxt(a1) - a1, nxt(a0) - a0
        both = jnp.where(last, (nxt(s1) - s1) * change1 + (nxt(s0) - s0) * change0, 0.0)
        fz = jnp.where(last, d * q * change0, 0.0)
        total += fz - pltpu.roll(fz, 1, 1)
        slopes += q * q * both + pltpu.roll(p * p * both, 1, 1)
        code = labels[x]
        bind, release = rate(code, bind_t), rate(code, release_t)
        b1 = 0.5 * a1 + release * (a1 - 0.5 * a1)
        grad[x] = -2.0 * slopes
        adjoint[0, x] = a0 + 2.0 * total + bind * (b1 - a0)
        adjoint[1, x] = b1 + release * (a0 - b1)


def swap_along_gy(shape, parity):
    nx, ny = shape
    pairs = []
    for i in range(nx):
        for j in range((parity + i) % 2, ny - 1, 2):
            a, b = i * ny + j, i * ny + j + 1
            pairs += [(a, b), (b, a)]
    return pairs


def shards(misfit, bleach_mask, labels, diffusion, bind_table, release_table, kern_x, kern_y, kern_z, free_states):
    nx, ny, depth = misfit.shape
    steps = free_states.shape[0]
    reach = (kern_x.shape[0] - 1) // 2
    width = reach + RIM
    tall = ny + 2 * RIM
    shape = (lax.axis_size("gx"), lax.axis_size("gy"))
    f32 = jnp.float32
    vmem = pl.BlockSpec(memory_space=pltpu.VMEM)
    smem = pl.BlockSpec(memory_space=pltpu.SMEM)
    params = pltpu.CompilerParams(vmem_limit_bytes=40 * 1024 * 1024)
    flat = (nx * ny, depth)

    slots = width + RIM + 1 + steps
    slab = jax.ShapeDtypeStruct((slots, nx, depth), f32)
    own, one, two = pl.pallas_call(
        functools.partial(first_kernel, reach),
        out_shape=[jax.ShapeDtypeStruct((ny, nx, depth), f32), slab, slab],
        in_specs=[vmem] * 6,
        out_specs=[vmem] * 3,
        scratch_shapes=[pltpu.VMEM((8, depth), f32), pltpu.VMEM(flat, f32), pltpu.VMEM((steps * nx * ny, depth), f32)],
        compiler_params=params,
        name="weigh_blur_z",
    )(misfit.reshape(flat), bleach_mask.reshape(flat), labels.reshape(flat), diffusion.reshape(flat), free_states,
      kern_z.reshape(1, -1))
    one = lax.ppermute(one, AXES, swap_along_gy(shape, 0))
    two = lax.ppermute(two, AXES, swap_along_gy(shape, 1))

    rows = (width + RIM) * tall + (1 + steps) * ny
    slab = jax.ShapeDtypeStruct((rows, depth), f32)
    blurred, outer, inner = pl.pallas_call(
        second_kernel,
        out_shape=[jax.ShapeDtypeStruct((nx * SLOT, depth), f32), slab, slab],
        in_specs=[vmem] * 6 + [smem],
        out_specs=[vmem] * 3,
        scratch_shapes=[pltpu.VMEM((ny + 2 * width, nx, depth), f32), pltpu.VMEM((2, slots - width, nx, depth), f32)],
        compiler_params=params,
        name="blur_y",
    )(own, one, two, labels, diffusion, free_states, kern_y)

    line = shape[1]
    across = []
    for i in range(1, shape[0] - 1, 2):
        for j in range(line):
            a, b = i * line + j, (i + 1) * line + j
            across += [(a, b), (b, a)]
    within = [[i * line + j, (i + 1) * line + j] for i in range(0, shape[0], 2) for j in range(line)]
    outer = lax.ppermute(outer, AXES, across)
    inner = lax.all_gather(inner, AXES, axis_index_groups=within)

    high = SLOT + 8
    grad, adjoint = pl.pallas_call(
        third_kernel,
        out_shape=[jax.ShapeDtypeStruct((nx, ny, depth), f32), jax.ShapeDtypeStruct((2, nx, ny, depth), f32)],
        in_specs=[vmem] * 8 + [smem] * 3,
        out_specs=[vmem] * 2,
        scratch_shapes=[
            pltpu.VMEM((nx + 2 * width, SLOT, depth), f32),
            pltpu.VMEM((nx + 2 * RIM, high, depth), f32),
            pltpu.VMEM((nx + 2, high, depth), f32),
            pltpu.VMEM((nx + 2 * RIM, high, depth), f32),
            pltpu.VMEM((steps, nx + 2, high, depth), f32),
            pltpu.VMEM((nx + 2, high, depth), f32),
        ],
        compiler_params=params,
        name="blur_x_steps",
    )(blurred, outer, inner, one, two, labels, diffusion, free_states, kern_x, bind_table, release_table)
    return grad, adjoint


def solution(mesh):
    tile = P("gx", "gy", None)
    in_specs = (tile, tile, tile, tile, P(), P(), P(), P(), P(), P(None, "gx", "gy", None))
    out_specs = (tile, P(None, "gx", "gy", None))
    return jax.shard_map(shards, mesh=mesh, in_specs=in_specs, out_specs=out_specs, check_vma=False)
```

```python
import functools

import jax
import jax.numpy as jnp
from jax import lax
from jax.experimental import pallas as pl
from jax.experimental.pallas import tpu as pltpu
from jax.sharding import PartitionSpec as P

AXES = ("gx", "gy")
RIM = 2
JOFF = 4
SLOT = 32
HIGH = 40
F32 = jnp.float32


def blur(read, write, taps, outs, sources, group=14, base=None):
    span = len(taps)
    for start in range(0, len(outs), group):
        mine = outs[start:start + group]
        acc = {i: base(i) for i in mine} if base else {}
        for e in sources:
            users = [i for i in mine if 0 <= e - i < span]
            if users:
                value = read(e)
            for i in users:
                term = taps[e - i] * value
                acc[i] = acc[i] + term if i in acc else term
        for i in mine:
            write(i, acc[i])


def right_comes_first():
    return (lax.axis_index("gx") + lax.axis_index("gy")) % 2 == 0


def is_even():
    return lax.axis_index("gx") % 2 == 0


def both_ways(flag, act):
    pl.when(flag)(functools.partial(act, True))
    pl.when(jnp.logical_not(flag))(functools.partial(act, False))


def first_kernel(reach, misfit_h, mask_h, labels_h, diffusion_h, states_h, kern_h, own, one, two,
                 misfit, mask, labels, diffusion, states, kern, work, edge, sems):
    steps, nx, ny, depth = states.shape
    copies = [pltpu.make_async_copy(a, b, sems.at[n]) for n, (a, b) in enumerate(
        ((kern_h, kern), (misfit_h, misfit), (mask_h, mask), (diffusion_h, diffusion), (labels_h, labels), (states_h, states)))]
    for c in copies:
        c.start()
    taps_z = kern.shape[0]
    half = (taps_z - 1) // 2
    copies[0].wait()
    lane = lax.broadcasted_iota(jnp.int32, (8, depth), 1)
    parts = [jnp.zeros((8, depth), F32) for _ in range(4)]
    for t in range(taps_z):
        parts[t % 4] = jnp.where(lane == t, kern[t], parts[t % 4])
    row = (parts[0] + parts[1]) + (parts[2] + parts[3])
    rolled = pltpu.roll(jnp.broadcast_to(row[0:1], (depth, depth)), depth - half, 1, stride=1, stride_axis=0)
    w = lax.broadcasted_iota(jnp.int32, (depth, depth), 0)
    z = lax.broadcasted_iota(jnp.int32, (depth, depth), 1)
    matrix = jnp.where(jnp.abs(z - w) <= half, rolled, 0.0)
    copies[1].wait()
    copies[2].wait()
    weighted = (1.0 + 3.0 * mask[...].astype(F32)) * misfit[...]
    work[...] = lax.dot_general(
        weighted, matrix, (((1,), (1,)), ((), ())),
        precision=lax.Precision.HIGHEST, preferred_element_type=F32)
    for c in copies[3:]:
        c.wait()
    edge[...] = states[...].astype(F32).reshape(edge.shape)
    octets = nx // 8
    for y in range(ny):
        for o in range(octets):
            own[y, pl.ds(8 * o, 8), :] = work[pl.ds(8 * o * ny + y, 8, stride=ny), :]
    width = reach + RIM

    def pack(out, right):
        start = ny - width if right else 0
        for y in range(width):
            out[y] = own[start + y]
        for k in range(RIM):
            y = ny - RIM + k if right else k
            for o in range(octets):
                out[width + k, pl.ds(8 * o, 8), :] = diffusion[pl.ds(8 * o * ny + y, 8, stride=ny), :]
        y = ny - 1 if right else 0
        for o in range(octets):
            here = pl.ds(8 * o * ny + y, 8, stride=ny)
            out[width + RIM, pl.ds(8 * o, 8), :] = labels[here, :].astype(F32)
            for s in range(steps):
                at = pl.ds((s * nx + 8 * o) * ny + y, 8, stride=ny)
                out[width + RIM + 1 + s, pl.ds(8 * o, 8), :] = edge[at, :]

    def act(right):
        pack(one, right)
        pack(two, not right)

    both_ways(right_comes_first(), act)


def own_y_kernel(own, kern_y, part):
    ny, nx, _ = own.shape
    taps = [kern_y[t] for t in range(kern_y.shape[0])]
    width = (len(taps) - 1) // 2 + RIM

    @pl.loop(0, nx // 8)
    def _(o):
        at = pl.ds(pl.multiple_of(8 * o, 8), 8)

        def write(j, value):
            part[j, at, :] = value

        blur(lambda e: own[e - width, at, :], write, taps, range(ny + 2 * RIM), range(width, width + ny))


def rest_y_kernel(part, one, two, labels, diffusion, states, kern_y, blurred, outer, inner, left, right):
    tall, nx, depth = part.shape
    ny = tall - 2 * RIM
    taps = [kern_y[t] for t in range(kern_y.shape[0])]
    width = (len(taps) - 1) // 2 + RIM

    def place(first):
        left[...] = (two if first else one)[...]
        right[...] = (one if first else two)[...]

    both_ways(right_comes_first(), place)

    for o in range(nx // 8):
        at = pl.ds(8 * o, 8)

        def read(e):
            return left[e, at, :] if e < width else right[e - width - ny, at, :]

        def write(j, value):
            blurred[pl.ds(8 * o * SLOT + JOFF - RIM + j, 8, stride=SLOT), :] = value

        blur(read, write, taps, range(tall), [*range(width), *range(width + ny, 2 * width + ny)],
             base=lambda j: part[j, at, :])

    def pack(out, upper):
        at = 0
        order = range(nx - 1, -1, -1) if upper else range(nx)
        for x in order[:width]:
            out[pl.ds(at, tall), :] = blurred[pl.ds(x * SLOT + JOFF - RIM, tall), :]
            at += tall
        for x in order[:RIM]:
            for r in range(RIM):
                out[pl.ds(at + r, 1), :] = left[width + r, pl.ds(x, 1), :]
                out[pl.ds(at + RIM + ny + r, 1), :] = right[width + r, pl.ds(x, 1), :]
            out[pl.ds(at + RIM, ny), :] = diffusion[x]
            at += tall
        x = order[0]
        out[pl.ds(at, ny), :] = labels[x].astype(F32)
        at += ny
        for s in range(states.shape[0]):
            out[pl.ds(at, ny), :] = states[s, x].astype(F32)
            at += ny

    def act(even):
        pack(inner, even)
        pack(outer, not even)

    both_ways(is_even(), act)


def rate(code, table):
    return jnp.where(code == 0, table[0], jnp.where(code == 1, table[1], table[2]))


def shares(here, there):
    inverse = 1.0 / jnp.maximum(here + there, 1e-30)
    return there * inverse, here * inverse


def inside(rows, depth):
    return lax.broadcasted_iota(jnp.int32, (rows, depth), 1) < depth - 1


def early_x_kernel(blurred, inner, one, two, labels, diffusion, states, kern_x, bind_t,
                   image, coef, state, keep, cx, cy, cz, xl, xu, yl, yu, zl, zu, ext, kind):
    nx, ny, depth = labels.shape
    steps = states.shape[0]
    taps = [kern_x[t] for t in range(kern_x.shape[0])]
    width = (len(taps) - 1) // 2 + RIM
    tall = ny + 2 * RIM
    lo, own_rows = JOFF - RIM, slice(JOFF, JOFF + ny)
    outs = range(nx + 2 * RIM)

    def place(even):
        slab = inner.at[1 if even else 0]
        at = 0
        for k in range(width):
            ext[k, lo:lo + tall, :] = slab[pl.ds(at, tall), :]
            at += tall
        first, step = (nx + RIM, 1) if even else (RIM - 1, -1)
        for k in range(RIM):
            coef[first + step * k, lo:lo + tall, :] = slab[pl.ds(at, tall), :]
            at += tall
        kind[first, own_rows, :] = slab[pl.ds(at, ny), :]
        at += ny
        for s in range(steps):
            state[s, first, own_rows, :] = slab[pl.ds(at, ny), :]
            at += ny

    both_ways(is_even(), place)

    for x in range(nx):
        p = RIM + x
        coef[p, own_rows, :] = diffusion[x]
        kind[p, own_rows, :] = labels[x].astype(F32)
        for s in range(steps):
            state[s, p, own_rows, :] = states[s, x].astype(F32)

    def rims(first):
        left, right = (two, one) if first else (one, two)
        for x in range(nx):
            p, row = RIM + x, pl.ds(x, 1)
            for k in range(RIM):
                coef[p, lo + k:lo + k + 1, :] = left[width + k, row, :]
                coef[p, JOFF + ny + k:JOFF + ny + k + 1, :] = right[width + k, row, :]
            kind[p, JOFF - 1:JOFF, :] = left[width + RIM, row, :]
            kind[p, JOFF + ny:JOFF + ny + 1, :] = right[width + RIM, row, :]
            for s in range(steps):
                state[s, p, JOFF - 1:JOFF, :] = left[width + RIM + 1 + s, row, :]
                state[s, p, JOFF + ny:JOFF + ny + 1, :] = right[width + RIM + 1 + s, row, :]

    both_ways(right_comes_first(), rims)

    @pl.loop(0, SLOT // 8)
    def _(v):
        rows = pl.ds(pl.multiple_of(8 * v, 8), 8)

        def write(i, value):
            image[i, rows, :] = value

        def near(e):
            return blurred[pl.ds(pl.multiple_of((e - width) * SLOT + 8 * v, 8), 8), :]

        blur(near, write, taps, outs, range(width, width + nx))

        def add(even):
            here = range(width + nx, 2 * width + nx) if even else range(width)
            touched = outs[nx + 2 * RIM - width:] if even else outs[:width]
            blur(lambda e: ext[e - width - nx if even else width - 1 - e, rows, :], write, taps, touched, here,
                 base=lambda i: image[i, rows, :])

        both_ways(is_even(), add)

    last = inside(SLOT, depth)

    @pl.loop(0, nx + 2 * RIM - 1)
    def _(p):
        h = slice(0, SLOT)
        d = coef[p, h, :]
        for there, c, low, up in ((coef[p + 1, h, :], cx, xl, xu), (coef[p, 1:SLOT + 1, :], cy, yl, yu),
                                  (pltpu.roll(d, depth - 1, 1), cz, zl, zu)):
            q, r = shares(d, there)
            if c is cz:
                q, r = jnp.where(last, q, 0.0), jnp.where(last, r, 0.0)
            c[p, h, :] = 2.0 * d * q
            low[p, h, :] = 2.0 * q * q
            up[p, h, :] = 2.0 * r * r
        keep[p, h, :] = 1.0 - 0.5 * rate(kind[p, h, :], bind_t)


def last_kernel(part, coef, state, keep, cx, cy, cz, xl, xu, yl, yu, zl, zu, outer, labels, kern_x, bind_t, release_t,
                grad_h, adjoint_h, ext, image, adj, rim, grad, adjoint, sems):
    nx, ny, depth = labels.shape
    steps = state.shape[0]
    taps = [kern_x[t] for t in range(kern_x.shape[0])]
    width = (len(taps) - 1) // 2 + RIM
    tall = ny + 2 * RIM
    lo, own_rows = JOFF - RIM, slice(JOFF, JOFF + ny)
    outs = range(nx + 2 * RIM)
    even = is_even()

    for k in range(width):
        ext[k, lo:lo + tall, :] = outer[pl.ds(k * tall, tall), :]
    for k in range(RIM):
        rim[k, lo:lo + tall, :] = outer[pl.ds((width + k) * tall, tall), :]
    tail = (width + RIM) * tall
    rim[RIM, own_rows, :] = outer[pl.ds(tail, ny), :]
    for s in range(steps):
        rim[RIM + 1 + s, own_rows, :] = outer[pl.ds(tail + (1 + s) * ny, ny), :]

    @pl.loop(0, SLOT // 8)
    def _(v):
        rows = pl.ds(pl.multiple_of(8 * v, 8), 8)

        def write(i, value):
            image[i, rows, :] = value

        def add(even):
            far = range(width) if even else range(width + nx, 2 * width + nx)
            touched = outs[:width] if even else outs[nx + 2 * RIM - width:]
            blur(lambda e: ext[width - 1 - e if even else e - width - nx, rows, :], write, taps, touched, far,
                 base=lambda i: part[i, rows, :])
            for i in outs:
                if i not in touched:
                    image[i, rows, :] = part[i, rows, :]

        both_ways(even, add)

    h = slice(JOFF - RIM, JOFF - RIM + SLOT)
    down = slice(h.start - 1, h.stop - 1)
    after = slice(h.start + 1, h.stop + 1)

    def first(p, c_low, c_up, c_y, c_y_low, c_z, kept):
        a = image[p, h, :]
        total = c_up * (image[p + 1, h, :] - a) + c_low * (image[p - 1, h, :] - a)
        total += c_y * (image[p, after, :] - a) + c_y_low * (image[p, down, :] - a)
        fz = c_z * (pltpu.roll(a, depth - 1, 1) - a)
        adj[p, h, :] = kept * a + total + (fz - pltpu.roll(fz, 1, 1))

    def coupling(here, there):
        q, _ = shares(here, there)
        return 2.0 * here * q

    before, next_ = slice(JOFF - 1, JOFF - 1 + ny), slice(JOFF + 1, JOFF + 1 + ny)

    def second(p, c_low, s_low, state_low, c_up, s_up, state_up):
        at = own_rows
        a1, a0 = image[p, at, :], adj[p, at, :]
        s1, s0 = state[steps - 1, p, at, :], state[0, p, at, :]
        total, slopes = 0.0, 0.0

        def face(c, s, i, rows, states):
            change1, change0 = image[i, rows, :] - a1, adj[i, rows, :] - a0
            return c * change0, s * ((states[0] - s1) * change1 + (states[1] - s0) * change0)

        x = p - RIM
        for f, g in (face(c_low, s_low, p - 1, at, state_low), face(c_up, s_up, p + 1, at, state_up),
                     face(cy[p, before, :], yu[p, before, :], p, before,
                          (state[steps - 1, p, before, :], state[0, p, before, :])),
                     face(cy[p, at, :], yl[p, at, :], p, next_, (state[steps - 1, p, next_, :], state[0, p, next_, :]))):
            total, slopes = total + f, slopes + g
        nxt = functools.partial(pltpu.roll, shift=depth - 1, axis=1)
        change1, change0 = nxt(a1) - a1, nxt(a0) - a0
        both = (nxt(s1) - s1) * change1 + (nxt(s0) - s0) * change0
        fz = cz[p, at, :] * change0
        total += fz - pltpu.roll(fz, 1, 1)
        slopes += zl[p, at, :] * both + pltpu.roll(zu[p, at, :] * both, 1, 1)
        code = labels[x]
        bind, release = rate(code, bind_t), rate(code, release_t)
        b1 = 0.5 * a1 + release * (a1 - 0.5 * a1)
        grad[x] = -slopes
        adjoint[0, x] = a0 + total + bind * (b1 - a0)
        adjoint[1, x] = b1 + release * (a0 - b1)

    def send(n, x, count):
        at = pl.ds(x, count)
        pairs = ((grad.at[at], grad_h.at[at]), (adjoint.at[0, at], adjoint_h.at[0, at]),
                 (adjoint.at[1, at], adjoint_h.at[1, at]))
        return [pltpu.make_async_copy(a, b, sems.at[n, m]) for m, (a, b) in enumerate(pairs)]

    def near_rim(even):
        near, far, tile = (1, 0, RIM) if even else (nx + RIM, nx + RIM + 1, nx + RIM - 1)
        d, d_far, d_tile = rim[0, h, :], rim[1, h, :], coef[tile, h, :]
        c_tile, c_far = coupling(d, d_tile), coupling(d, d_far)
        c_z = jnp.where(inside(SLOT, depth), coupling(d, pltpu.roll(d, depth - 1, 1)), 0.0)
        kept = 1.0 - 0.5 * rate(rim[RIM, h, :], bind_t)
        c_low, c_up = (c_far, c_tile) if even else (c_tile, c_far)
        first(near, c_low, c_up, coupling(d, rim[0, after, :]), coupling(d, rim[0, down, :]), c_z, kept)
        inner_face = cx[tile, h, :] if even else cx[tile - 1, h, :]
        c_low, c_up = (c_tile, inner_face) if even else (inner_face, c_tile)
        first(tile, c_low, c_up, cy[tile, h, :], cy[tile, down, :], cz[tile, h, :], keep[tile, h, :])

    def near_rim_second(even):
        tile = RIM if even else nx + RIM - 1
        at = own_rows
        q, r = shares(coef[tile, at, :], rim[0, at, :])
        far = (2.0 * coef[tile, at, :] * q, 2.0 * q * q, (rim[RIM + steps, at, :], rim[RIM + 1, at, :]))
        if even:
            second(tile, *far, cx[tile, at, :], xl[tile, at, :],
                   (state[steps - 1, tile + 1, at, :], state[0, tile + 1, at, :]))
        else:
            second(tile, cx[tile - 1, at, :], xu[tile - 1, at, :],
                   (state[steps - 1, tile - 1, at, :], state[0, tile - 1, at, :]), *far)

    both_ways(even, near_rim)

    @pl.loop(0, nx)
    def _(n):
        p = n + jnp.where(even, RIM + 1, 1)
        first(p, cx[p - 1, h, :], cx[p, h, :], cy[p, h, :], cy[p, down, :], cz[p, h, :], keep[p, h, :])

    both_ways(even, near_rim_second)
    copies = send(0, jnp.where(even, 0, nx - 1), 1)
    for c in copies:
        c.start()
    base = jnp.where(even, RIM + 1, RIM)
    size = -(-(nx - 1) // 3)
    for n in range(3):
        count = min(size, nx - 1 - n * size)

        @pl.loop(n * size, n * size + count)
        def _(k):
            p = base + k
            at = own_rows
            second(p, cx[p - 1, at, :], xu[p - 1, at, :], (state[steps - 1, p - 1, at, :], state[0, p - 1, at, :]),
                   cx[p, at, :], xl[p, at, :], (state[steps - 1, p + 1, at, :], state[0, p + 1, at, :]))

        more = send(n + 1, base - RIM + n * size, count)
        for c in more:
            c.start()
        copies += more
    for c in copies:
        c.wait()


def swap_along_gy(shape, parity):
    nx, ny = shape
    pairs = []
    for i in range(nx):
        for j in range((parity + i) % 2, ny - 1, 2):
            a, b = i * ny + j, i * ny + j + 1
            pairs += [(a, b), (b, a)]
    return pairs


def shards(misfit, bleach_mask, labels, diffusion, bind_table, release_table, kern_x, kern_y, kern_z, free_states):
    nx, ny, depth = misfit.shape
    steps = free_states.shape[0]
    reach = (kern_x.shape[0] - 1) // 2
    width = reach + RIM
    tall = ny + 2 * RIM
    shape = (lax.axis_size("gx"), lax.axis_size("gy"))
    vmem = pl.BlockSpec(memory_space=pltpu.VMEM)
    smem = pl.BlockSpec(memory_space=pltpu.SMEM)
    hbm = pl.BlockSpec(memory_space=pl.ANY)
    params = pltpu.CompilerParams(vmem_limit_bytes=24 * 1024 * 1024)
    flat = (nx * ny, depth)
    array = jax.ShapeDtypeStruct

    def in_hbm(x):
        return pltpu.with_memory_space_constraint(x, pltpu.MemorySpace.HBM)

    slots = width + RIM + 1 + steps
    slab = array((slots, nx, depth), F32)
    own, one, two = pl.pallas_call(
        functools.partial(first_kernel, reach),
        out_shape=[array((ny, nx, depth), F32), slab, slab],
        in_specs=[hbm] * 6,
        out_specs=[vmem] * 3,
        scratch_shapes=[
            pltpu.VMEM(flat, F32), pltpu.VMEM(flat, jnp.int32), pltpu.VMEM(flat, jnp.int32), pltpu.VMEM(flat, F32),
            pltpu.VMEM(free_states.shape, free_states.dtype), pltpu.SMEM(kern_z.shape, F32),
            pltpu.VMEM(flat, F32), pltpu.VMEM((steps * nx * ny, depth), F32), pltpu.SemaphoreType.DMA((6,))],
        compiler_params=params,
        name="weigh_blur_z",
    )(in_hbm(misfit.reshape(flat)), in_hbm(bleach_mask.reshape(flat)), in_hbm(labels.reshape(flat)),
      in_hbm(diffusion.reshape(flat)), in_hbm(free_states), in_hbm(kern_z))
    one = lax.ppermute(one, AXES, swap_along_gy(shape, 0))
    two = lax.ppermute(two, AXES, swap_along_gy(shape, 1))

    part = pl.pallas_call(
        own_y_kernel,
        out_shape=array((tall, nx, depth), F32),
        in_specs=[vmem, smem],
        out_specs=vmem,
        compiler_params=params,
        cost_estimate=pl.CostEstimate(flops=4_000_000, bytes_accessed=700_000, transcendentals=0),
        name="own_y",
    )(own, kern_y)

    rows = (width + RIM) * tall + (1 + steps) * ny
    slab = array((rows, depth), F32)
    blurred, outer, inner = pl.pallas_call(
        rest_y_kernel,
        out_shape=[array((nx * SLOT, depth), F32), slab, slab],
        in_specs=[vmem] * 6 + [smem],
        out_specs=[vmem] * 3,
        scratch_shapes=[pltpu.VMEM((slots, nx, depth), F32)] * 2,
        compiler_params=params,
        name="rest_y",
    )(part, one, two, labels, diffusion, free_states, kern_y)

    line = shape[1]
    across = []
    for i in range(1, shape[0] - 1, 2):
        for j in range(line):
            a, b = i * line + j, (i + 1) * line + j
            across += [(a, b), (b, a)]
    within = [[i * line + j, (i + 1) * line + j] for i in range(0, shape[0], 2) for j in range(line)]
    outer = lax.ppermute(outer, AXES, across)
    inner = lax.all_gather(inner, AXES, axis_index_groups=within)

    around = (nx + 2 * RIM, HIGH, depth)
    field = array(around, F32)
    early = pl.pallas_call(
        early_x_kernel,
        out_shape=[field, field, array((steps, *around), F32)] + [field] * 10,
        in_specs=[vmem] * 7 + [smem] * 2,
        out_specs=[vmem] * 13,
        scratch_shapes=[pltpu.VMEM((width, SLOT, depth), F32), pltpu.VMEM(around, F32)],
        compiler_params=params,
        cost_estimate=pl.CostEstimate(flops=8_000_000, bytes_accessed=3_000_000, transcendentals=0),
        name="early_x",
    )(blurred, inner, one, two, labels, diffusion, free_states, kern_x, bind_table)

    tile = (nx, ny, depth)
    grad, adjoint = pl.pallas_call(
        last_kernel,
        out_shape=[array(tile, F32), array((2, *tile), F32)],
        in_specs=[vmem] * 15 + [smem] * 3,
        out_specs=[hbm] * 2,
        scratch_shapes=[
            pltpu.VMEM((width, SLOT, depth), F32),
            pltpu.VMEM(around, F32),
            pltpu.VMEM(around, F32),
            pltpu.VMEM((RIM + 1 + steps, HIGH, depth), F32),
            pltpu.VMEM(tile, F32),
            pltpu.VMEM((2, *tile), F32),
            pltpu.SemaphoreType.DMA((4, 3)),
        ],
        compiler_params=params,
        name="late_x_steps",
    )(*early, outer, labels, kern_x, bind_table, release_table)
    return grad, adjoint


def solution(mesh):
    tile = P("gx", "gy", None)
    in_specs = (tile, tile, tile, tile, P(), P(), P(), P(), P(), P(None, "gx", "gy", None))
    out_specs = (tile, P(None, "gx", "gy", None))
    return jax.shard_map(shards, mesh=mesh, in_specs=in_specs, out_specs=out_specs, check_vma=False)
```

```python
import functools

import jax
import jax.numpy as jnp
from jax import lax
from jax.experimental import pallas as pl
from jax.experimental.pallas import tpu as pltpu
from jax.sharding import PartitionSpec as P

AXES = ("gx", "gy")
RIM = 2
JOFF = 4
SLOT = 32
HIGH = 40
CHUNKS = 4
F32 = jnp.float32


def blur(read, write, taps, outs, sources, group=14, base=None):
    span = len(taps)
    for start in range(0, len(outs), group):
        mine = outs[start:start + group]
        acc = {i: base(i) for i in mine} if base else {}
        for e in sources:
            users = [i for i in mine if 0 <= e - i < span]
            if users:
                value = read(e)
            for i in users:
                term = taps[e - i] * value
                acc[i] = acc[i] + term if i in acc else term
        for i in mine:
            write(i, acc[i])


def right_comes_first():
    return (lax.axis_index("gx") + lax.axis_index("gy")) % 2 == 0


def is_even():
    return lax.axis_index("gx") % 2 == 0


def both_ways(flag, act):
    pl.when(flag)(functools.partial(act, True))
    pl.when(jnp.logical_not(flag))(functools.partial(act, False))


def first_kernel(reach, misfit_h, mask_h, labels_h, diffusion_h, states_h, kern_h, own, one, two,
                 misfit, mask, labels, diffusion, states, kern, work, edge, sems):
    steps, nx, ny, depth = states.shape
    copies = [pltpu.make_async_copy(a, b, sems.at[n]) for n, (a, b) in enumerate(
        ((kern_h, kern), (misfit_h, misfit), (mask_h, mask), (diffusion_h, diffusion), (labels_h, labels), (states_h, states)))]
    for c in copies:
        c.start()
    taps_z = kern.shape[0]
    half = (taps_z - 1) // 2
    copies[0].wait()
    lane = lax.broadcasted_iota(jnp.int32, (8, depth), 1)
    parts = [jnp.zeros((8, depth), F32) for _ in range(4)]
    for t in range(taps_z):
        parts[t % 4] = jnp.where(lane == t, kern[t], parts[t % 4])
    row = (parts[0] + parts[1]) + (parts[2] + parts[3])
    rolled = pltpu.roll(jnp.broadcast_to(row[0:1], (depth, depth)), depth - half, 1, stride=1, stride_axis=0)
    w = lax.broadcasted_iota(jnp.int32, (depth, depth), 0)
    z = lax.broadcasted_iota(jnp.int32, (depth, depth), 1)
    matrix = jnp.where(jnp.abs(z - w) <= half, rolled, 0.0)
    copies[1].wait()
    copies[2].wait()
    weighted = (1.0 + 3.0 * mask[...].astype(F32)) * misfit[...]
    work[...] = lax.dot_general(
        weighted, matrix, (((1,), (1,)), ((), ())),
        precision=lax.Precision.HIGHEST, preferred_element_type=F32)
    for c in copies[3:]:
        c.wait()
    edge[...] = states[...].astype(F32).reshape(edge.shape)
    octets = nx // 8
    for y in range(ny):
        for o in range(octets):
            own[y, pl.ds(8 * o, 8), :] = work[pl.ds(8 * o * ny + y, 8, stride=ny), :]
    width = reach + RIM

    def pack(out, right):
        start = ny - width if right else 0
        for y in range(width):
            out[y] = own[start + y]
        for k in range(RIM):
            y = ny - RIM + k if right else k
            for o in range(octets):
                out[width + k, pl.ds(8 * o, 8), :] = diffusion[pl.ds(8 * o * ny + y, 8, stride=ny), :]
        y = ny - 1 if right else 0
        for o in range(octets):
            here = pl.ds(8 * o * ny + y, 8, stride=ny)
            out[width + RIM, pl.ds(8 * o, 8), :] = labels[here, :].astype(F32)
            for s in range(steps):
                at = pl.ds((s * nx + 8 * o) * ny + y, 8, stride=ny)
                out[width + RIM + 1 + s, pl.ds(8 * o, 8), :] = edge[at, :]

    def act(right):
        pack(one, right)
        pack(two, not right)

    both_ways(right_comes_first(), act)


def own_y_kernel(own, kern_y, part):
    ny, nx, _ = own.shape
    taps = [kern_y[t] for t in range(kern_y.shape[0])]
    width = (len(taps) - 1) // 2 + RIM

    @pl.loop(0, nx // 8)
    def _(o):
        at = pl.ds(pl.multiple_of(8 * o, 8), 8)

        def write(j, value):
            part[j, at, :] = value

        blur(lambda e: own[e - width, at, :], write, taps, range(ny + 2 * RIM), range(width, width + ny))


def rest_y_kernel(part, one, two, labels, diffusion, states, kern_y, blurred, outer, inner, left, right):
    tall, nx, depth = part.shape
    ny = tall - 2 * RIM
    taps = [kern_y[t] for t in range(kern_y.shape[0])]
    width = (len(taps) - 1) // 2 + RIM

    def place(first):
        left[...] = (two if first else one)[...]
        right[...] = (one if first else two)[...]

    both_ways(right_comes_first(), place)

    for o in range(nx // 8):
        at = pl.ds(8 * o, 8)

        def read(e):
            return left[e, at, :] if e < width else right[e - width - ny, at, :]

        def write(j, value):
            blurred[pl.ds(8 * o * SLOT + JOFF - RIM + j, 8, stride=SLOT), :] = value

        blur(read, write, taps, range(tall), [*range(width), *range(width + ny, 2 * width + ny)],
             base=lambda j: part[j, at, :])

    def pack(out, upper):
        at = 0
        order = range(nx - 1, -1, -1) if upper else range(nx)
        for x in order[:width]:
            out[pl.ds(at, tall), :] = blurred[pl.ds(x * SLOT + JOFF - RIM, tall), :]
            at += tall
        for x in order[:RIM]:
            for r in range(RIM):
                out[pl.ds(at + r, 1), :] = left[width + r, pl.ds(x, 1), :]
                out[pl.ds(at + RIM + ny + r, 1), :] = right[width + r, pl.ds(x, 1), :]
            out[pl.ds(at + RIM, ny), :] = diffusion[x]
            at += tall
        x = order[0]
        out[pl.ds(at, ny), :] = labels[x].astype(F32)
        at += ny
        for s in range(states.shape[0]):
            out[pl.ds(at, ny), :] = states[s, x].astype(F32)
            at += ny

    def act(even):
        pack(inner, even)
        pack(outer, not even)

    both_ways(is_even(), act)


def rate(code, table):
    return jnp.where(code == 0, table[0], jnp.where(code == 1, table[1], table[2]))


def shares(here, there):
    inverse = 1.0 / jnp.maximum(here + there, 1e-30)
    return there * inverse, here * inverse


def inside(rows, depth):
    return lax.broadcasted_iota(jnp.int32, (rows, depth), 1) < depth - 1


def early_x_kernel(blurred, inner, one, two, labels, diffusion, states, kern_x, bind_t,
                   image, coef, state, keep, cx, cy, cz, xl, xu, yl, yu, zl, zu, ext, kind):
    nx, ny, depth = labels.shape
    steps = states.shape[0]
    taps = [kern_x[t] for t in range(kern_x.shape[0])]
    width = (len(taps) - 1) // 2 + RIM
    tall = ny + 2 * RIM
    lo, own_rows = JOFF - RIM, slice(JOFF, JOFF + ny)
    outs = range(nx + 2 * RIM)

    def place(even):
        slab = inner.at[1 if even else 0]
        at = 0
        for k in range(width):
            ext[k, lo:lo + tall, :] = slab[pl.ds(at, tall), :]
            at += tall
        first, step = (nx + RIM, 1) if even else (RIM - 1, -1)
        for k in range(RIM):
            coef[first + step * k, lo:lo + tall, :] = slab[pl.ds(at, tall), :]
            at += tall
        kind[first, own_rows, :] = slab[pl.ds(at, ny), :]
        at += ny
        for s in range(steps):
            state[s, first, own_rows, :] = slab[pl.ds(at, ny), :]
            at += ny

    both_ways(is_even(), place)

    for x in range(nx):
        p = RIM + x
        coef[p, own_rows, :] = diffusion[x]
        kind[p, own_rows, :] = labels[x].astype(F32)
        for s in range(steps):
            state[s, p, own_rows, :] = states[s, x].astype(F32)

    def rims(first):
        left, right = (two, one) if first else (one, two)
        for x in range(nx):
            p, row = RIM + x, pl.ds(x, 1)
            for k in range(RIM):
                coef[p, lo + k:lo + k + 1, :] = left[width + k, row, :]
                coef[p, JOFF + ny + k:JOFF + ny + k + 1, :] = right[width + k, row, :]
            kind[p, JOFF - 1:JOFF, :] = left[width + RIM, row, :]
            kind[p, JOFF + ny:JOFF + ny + 1, :] = right[width + RIM, row, :]
            for s in range(steps):
                state[s, p, JOFF - 1:JOFF, :] = left[width + RIM + 1 + s, row, :]
                state[s, p, JOFF + ny:JOFF + ny + 1, :] = right[width + RIM + 1 + s, row, :]

    both_ways(right_comes_first(), rims)

    @pl.loop(0, SLOT // 8)
    def _(v):
        rows = pl.ds(pl.multiple_of(8 * v, 8), 8)

        def write(i, value):
            image[i, rows, :] = value

        def near(e):
            return blurred[pl.ds(pl.multiple_of((e - width) * SLOT + 8 * v, 8), 8), :]

        blur(near, write, taps, outs, range(width, width + nx))

        def add(even):
            here = range(width + nx, 2 * width + nx) if even else range(width)
            touched = outs[nx + 2 * RIM - width:] if even else outs[:width]
            blur(lambda e: ext[e - width - nx if even else width - 1 - e, rows, :], write, taps, touched, here,
                 base=lambda i: image[i, rows, :])

        both_ways(is_even(), add)

    last = inside(SLOT, depth)

    @pl.loop(0, nx + 2 * RIM - 1, unroll=9)
    def _(p):
        h = slice(0, SLOT)
        d = coef[p, h, :]
        for there, c, low, up in ((coef[p + 1, h, :], cx, xl, xu), (coef[p, 1:SLOT + 1, :], cy, yl, yu),
                                  (pltpu.roll(d, depth - 1, 1), cz, zl, zu)):
            q, r = shares(d, there)
            if c is cz:
                q, r = jnp.where(last, q, 0.0), jnp.where(last, r, 0.0)
            c[p, h, :] = 2.0 * d * q
            low[p, h, :] = 2.0 * q * q
            up[p, h, :] = 2.0 * r * r
        keep[p, h, :] = 1.0 - 0.5 * rate(kind[p, h, :], bind_t)


def last_kernel(part, coef, state, keep, cx, cy, cz, xl, xu, yl, yu, zl, zu, outer, labels, kern_x, bind_t, release_t,
                grad_h, adjoint_h, ext, image, adj, rim, grad, adjoint, sems):
    nx, ny, depth = labels.shape
    steps = state.shape[0]
    taps = [kern_x[t] for t in range(kern_x.shape[0])]
    width = (len(taps) - 1) // 2 + RIM
    tall = ny + 2 * RIM
    lo, own_rows = JOFF - RIM, slice(JOFF, JOFF + ny)
    outs = range(nx + 2 * RIM)
    even = is_even()

    for k in range(width):
        ext[k, lo:lo + tall, :] = outer[pl.ds(k * tall, tall), :]
    for k in range(RIM):
        rim[k, lo:lo + tall, :] = outer[pl.ds((width + k) * tall, tall), :]
    tail = (width + RIM) * tall
    rim[RIM, own_rows, :] = outer[pl.ds(tail, ny), :]
    for s in range(steps):
        rim[RIM + 1 + s, own_rows, :] = outer[pl.ds(tail + (1 + s) * ny, ny), :]

    @pl.loop(0, SLOT // 8)
    def _(v):
        rows = pl.ds(pl.multiple_of(8 * v, 8), 8)

        def write(i, value):
            image[i, rows, :] = value

        def add(even):
            far = range(width) if even else range(width + nx, 2 * width + nx)
            touched = outs[:width] if even else outs[nx + 2 * RIM - width:]
            blur(lambda e: ext[width - 1 - e if even else e - width - nx, rows, :], write, taps, touched, far,
                 base=lambda i: part[i, rows, :])
            for i in outs:
                if i not in touched:
                    image[i, rows, :] = part[i, rows, :]

        both_ways(even, add)

    h = slice(JOFF - RIM, JOFF - RIM + SLOT)
    down = slice(h.start - 1, h.stop - 1)
    after = slice(h.start + 1, h.stop + 1)

    def first(p, c_low, c_up, c_y, c_y_low, c_z, kept):
        a = image[p, h, :]
        total = c_up * (image[p + 1, h, :] - a) + c_low * (image[p - 1, h, :] - a)
        total += c_y * (image[p, after, :] - a) + c_y_low * (image[p, down, :] - a)
        fz = c_z * (pltpu.roll(a, depth - 1, 1) - a)
        adj[p, h, :] = kept * a + total + (fz - pltpu.roll(fz, 1, 1))

    def coupling(here, there):
        q, _ = shares(here, there)
        return 2.0 * here * q

    before, next_ = slice(JOFF - 1, JOFF - 1 + ny), slice(JOFF + 1, JOFF + 1 + ny)

    def second(p, c_low, s_low, state_low, c_up, s_up, state_up):
        at = own_rows
        a1, a0 = image[p, at, :], adj[p, at, :]
        s1, s0 = state[steps - 1, p, at, :], state[0, p, at, :]
        total, slopes = 0.0, 0.0

        def face(c, s, i, rows, states):
            change1, change0 = image[i, rows, :] - a1, adj[i, rows, :] - a0
            return c * change0, s * ((states[0] - s1) * change1 + (states[1] - s0) * change0)

        x = p - RIM
        for f, g in (face(c_low, s_low, p - 1, at, state_low), face(c_up, s_up, p + 1, at, state_up),
                     face(cy[p, before, :], yu[p, before, :], p, before,
                          (state[steps - 1, p, before, :], state[0, p, before, :])),
                     face(cy[p, at, :], yl[p, at, :], p, next_, (state[steps - 1, p, next_, :], state[0, p, next_, :]))):
            total, slopes = total + f, slopes + g
        nxt = functools.partial(pltpu.roll, shift=depth - 1, axis=1)
        change1, change0 = nxt(a1) - a1, nxt(a0) - a0
        both = (nxt(s1) - s1) * change1 + (nxt(s0) - s0) * change0
        fz = cz[p, at, :] * change0
        total += fz - pltpu.roll(fz, 1, 1)
        slopes += zl[p, at, :] * both + pltpu.roll(zu[p, at, :] * both, 1, 1)
        code = labels[x]
        bind, release = rate(code, bind_t), rate(code, release_t)
        b1 = 0.5 * a1 + release * (a1 - 0.5 * a1)
        grad[x] = -slopes
        adjoint[0, x] = a0 + total + bind * (b1 - a0)
        adjoint[1, x] = b1 + release * (a0 - b1)

    def send(n, x, count):
        at = pl.ds(x, count)
        pairs = ((grad.at[at], grad_h.at[at]), (adjoint.at[0, at], adjoint_h.at[0, at]),
                 (adjoint.at[1, at], adjoint_h.at[1, at]))
        return [pltpu.make_async_copy(a, b, sems.at[n, m]) for m, (a, b) in enumerate(pairs)]

    def near_rim(even):
        near, far, tile = (1, 0, RIM) if even else (nx + RIM, nx + RIM + 1, nx + RIM - 1)
        d, d_far, d_tile = rim[0, h, :], rim[1, h, :], coef[tile, h, :]
        c_tile, c_far = coupling(d, d_tile), coupling(d, d_far)
        c_z = jnp.where(inside(SLOT, depth), coupling(d, pltpu.roll(d, depth - 1, 1)), 0.0)
        kept = 1.0 - 0.5 * rate(rim[RIM, h, :], bind_t)
        c_low, c_up = (c_far, c_tile) if even else (c_tile, c_far)
        first(near, c_low, c_up, coupling(d, rim[0, after, :]), coupling(d, rim[0, down, :]), c_z, kept)
        inner_face = cx[tile, h, :] if even else cx[tile - 1, h, :]
        c_low, c_up = (c_tile, inner_face) if even else (inner_face, c_tile)
        first(tile, c_low, c_up, cy[tile, h, :], cy[tile, down, :], cz[tile, h, :], keep[tile, h, :])

    def near_rim_second(even):
        tile = RIM if even else nx + RIM - 1
        at = own_rows
        q, r = shares(coef[tile, at, :], rim[0, at, :])
        far = (2.0 * coef[tile, at, :] * q, 2.0 * q * q, (rim[RIM + steps, at, :], rim[RIM + 1, at, :]))
        if even:
            second(tile, *far, cx[tile, at, :], xl[tile, at, :],
                   (state[steps - 1, tile + 1, at, :], state[0, tile + 1, at, :]))
        else:
            second(tile, cx[tile - 1, at, :], xu[tile - 1, at, :],
                   (state[steps - 1, tile - 1, at, :], state[0, tile - 1, at, :]), *far)

    both_ways(even, near_rim)

    @pl.loop(0, nx, unroll=8)
    def _(n):
        p = n + jnp.where(even, RIM + 1, 1)
        first(p, cx[p - 1, h, :], cx[p, h, :], cy[p, h, :], cy[p, down, :], cz[p, h, :], keep[p, h, :])

    both_ways(even, near_rim_second)
    copies = send(0, jnp.where(even, 0, nx - 1), 1)
    for c in copies:
        c.start()
    base = jnp.where(even, RIM + 1, RIM)
    size = -(-(nx - 1) // CHUNKS)
    for n in range(CHUNKS):
        count = min(size, nx - 1 - n * size)

        @pl.loop(n * size, n * size + count, unroll=count)
        def _(k):
            p = base + k
            at = own_rows
            second(p, cx[p - 1, at, :], xu[p - 1, at, :], (state[steps - 1, p - 1, at, :], state[0, p - 1, at, :]),
                   cx[p, at, :], xl[p, at, :], (state[steps - 1, p + 1, at, :], state[0, p + 1, at, :]))

        more = send(n + 1, base - RIM + n * size, count)
        for c in more:
            c.start()
        copies += more
    for c in copies:
        c.wait()


def swap_along_gy(shape, parity):
    nx, ny = shape
    pairs = []
    for i in range(nx):
        for j in range((parity + i) % 2, ny - 1, 2):
            a, b = i * ny + j, i * ny + j + 1
            pairs += [(a, b), (b, a)]
    return pairs


def shards(misfit, bleach_mask, labels, diffusion, bind_table, release_table, kern_x, kern_y, kern_z, free_states):
    nx, ny, depth = misfit.shape
    steps = free_states.shape[0]
    reach = (kern_x.shape[0] - 1) // 2
    width = reach + RIM
    tall = ny + 2 * RIM
    shape = (lax.axis_size("gx"), lax.axis_size("gy"))
    vmem = pl.BlockSpec(memory_space=pltpu.VMEM)
    smem = pl.BlockSpec(memory_space=pltpu.SMEM)
    hbm = pl.BlockSpec(memory_space=pl.ANY)
    params = pltpu.CompilerParams(vmem_limit_bytes=24 * 1024 * 1024)
    flat = (nx * ny, depth)
    array = jax.ShapeDtypeStruct

    def in_hbm(x):
        return pltpu.with_memory_space_constraint(x, pltpu.MemorySpace.HBM)

    slots = width + RIM + 1 + steps
    slab = array((slots, nx, depth), F32)
    own, one, two = pl.pallas_call(
        functools.partial(first_kernel, reach),
        out_shape=[array((ny, nx, depth), F32), slab, slab],
        in_specs=[hbm] * 6,
        out_specs=[vmem] * 3,
        scratch_shapes=[
            pltpu.VMEM(flat, F32), pltpu.VMEM(flat, jnp.int32), pltpu.VMEM(flat, jnp.int32), pltpu.VMEM(flat, F32),
            pltpu.VMEM(free_states.shape, free_states.dtype), pltpu.SMEM(kern_z.shape, F32),
            pltpu.VMEM(flat, F32), pltpu.VMEM((steps * nx * ny, depth), F32), pltpu.SemaphoreType.DMA((6,))],
        compiler_params=params,
        name="weigh_blur_z",
    )(in_hbm(misfit.reshape(flat)), in_hbm(bleach_mask.reshape(flat)), in_hbm(labels.reshape(flat)),
      in_hbm(diffusion.reshape(flat)), in_hbm(free_states), in_hbm(kern_z))
    one = lax.ppermute(one, AXES, swap_along_gy(shape, 0))
    two = lax.ppermute(two, AXES, swap_along_gy(shape, 1))

    part = pl.pallas_call(
        own_y_kernel,
        out_shape=array((tall, nx, depth), F32),
        in_specs=[vmem, smem],
        out_specs=vmem,
        compiler_params=params,
        cost_estimate=pl.CostEstimate(flops=4_000_000, bytes_accessed=700_000, transcendentals=0),
        name="own_y",
    )(own, kern_y)

    rows = (width + RIM) * tall + (1 + steps) * ny
    slab = array((rows, depth), F32)
    blurred, outer, inner = pl.pallas_call(
        rest_y_kernel,
        out_shape=[array((nx * SLOT, depth), F32), slab, slab],
        in_specs=[vmem] * 6 + [smem],
        out_specs=[vmem] * 3,
        scratch_shapes=[pltpu.VMEM((slots, nx, depth), F32)] * 2,
        compiler_params=params,
        name="rest_y",
    )(part, one, two, labels, diffusion, free_states, kern_y)

    line = shape[1]
    across = []
    for i in range(1, shape[0] - 1, 2):
        for j in range(line):
            a, b = i * line + j, (i + 1) * line + j
            across += [(a, b), (b, a)]
    within = [[i * line + j, (i + 1) * line + j] for i in range(0, shape[0], 2) for j in range(line)]
    outer = lax.ppermute(outer, AXES, across)
    inner = lax.all_gather(inner, AXES, axis_index_groups=within)

    around = (nx + 2 * RIM, HIGH, depth)
    field = array(around, F32)
    early = pl.pallas_call(
        early_x_kernel,
        out_shape=[field, field, array((steps, *around), F32)] + [field] * 10,
        in_specs=[vmem] * 7 + [smem] * 2,
        out_specs=[vmem] * 13,
        scratch_shapes=[pltpu.VMEM((width, SLOT, depth), F32), pltpu.VMEM(around, F32)],
        compiler_params=params,
        cost_estimate=pl.CostEstimate(flops=8_000_000, bytes_accessed=3_000_000, transcendentals=0),
        name="early_x",
    )(blurred, inner, one, two, labels, diffusion, free_states, kern_x, bind_table)

    tile = (nx, ny, depth)
    grad, adjoint = pl.pallas_call(
        last_kernel,
        out_shape=[array(tile, F32), array((2, *tile), F32)],
        in_specs=[vmem] * 15 + [smem] * 3,
        out_specs=[hbm] * 2,
        scratch_shapes=[
            pltpu.VMEM((width, SLOT, depth), F32),
            pltpu.VMEM(around, F32),
            pltpu.VMEM(around, F32),
            pltpu.VMEM((RIM + 1 + steps, HIGH, depth), F32),
            pltpu.VMEM(tile, F32),
            pltpu.VMEM((2, *tile), F32),
            pltpu.SemaphoreType.DMA((CHUNKS + 1, 3)),
        ],
        compiler_params=params,
        name="late_x_steps",
    )(*early, outer, labels, kern_x, bind_table, release_table)
    return grad, adjoint


def solution(mesh):
    tile = P("gx", "gy", None)
    in_specs = (tile, tile, tile, tile, P(), P(), P(), P(), P(), P(None, "gx", "gy", None))
    out_specs = (tile, P(None, "gx", "gy", None))
    return jax.shard_map(shards, mesh=mesh, in_specs=in_specs, out_specs=out_specs, check_vma=False)
```

```python
import functools

import jax
import jax.numpy as jnp
from jax import lax
from jax.experimental import pallas as pl
from jax.experimental.pallas import tpu as pltpu
from jax.sharding import PartitionSpec as P

AXES = ("gx", "gy")
RIM = 2
JOFF = 4
SLOT = 32
HIGH = 40
CHUNKS = 4
F32 = jnp.float32


def blur(read, write, taps, outs, sources, group=14, base=None):
    span = len(taps)
    for start in range(0, len(outs), group):
        mine = outs[start:start + group]
        acc = {i: base(i) for i in mine} if base else {}
        for e in sources:
            users = [i for i in mine if 0 <= e - i < span]
            if users:
                value = read(e)
            for i in users:
                term = taps[e - i] * value
                acc[i] = acc[i] + term if i in acc else term
        for i in mine:
            write(i, acc[i])


def vectors(spread, reach):
    span = 2 * reach + 1
    taps_x, taps_y, bind = range(span), range(span, 2 * span), 2 * span
    kinds = (spread.shape[0] - bind) // 2
    return taps_x, taps_y, range(bind, bind + kinds), range(bind + kinds, bind + 2 * kinds)


def right_comes_first():
    return (lax.axis_index("gx") + lax.axis_index("gy")) % 2 == 1


def is_even():
    return lax.axis_index("gx") % 2 == 0


def both_ways(flag, act):
    pl.when(flag)(functools.partial(act, True))
    pl.when(jnp.logical_not(flag))(functools.partial(act, False))


def first_kernel(reach, misfit_h, mask_h, labels_h, diffusion_h, states_h, kern_h, *rest):
    few_h, rest = rest[:4], rest[4:]
    own, one, two, spread, misfit, mask, labels, diffusion, states, kern, work, edge, *few, sems = rest
    steps, nx, ny, depth = states.shape
    copies = [pltpu.make_async_copy(a, b, sems.at[n]) for n, (a, b) in enumerate(
        ((kern_h, kern), (misfit_h, misfit), (mask_h, mask), (diffusion_h, diffusion), (labels_h, labels), (states_h, states), *zip(few_h, few)))]
    for c in copies[:3] + copies[6:] + copies[3:6]:
        c.start()
    taps_z = kern.shape[0]
    half = (taps_z - 1) // 2
    copies[0].wait()
    lane = lax.broadcasted_iota(jnp.int32, (8, depth), 1)
    parts = [jnp.zeros((8, depth), F32) for _ in range(4)]
    for t in range(taps_z):
        parts[t % 4] = jnp.where(lane == t, kern[t], parts[t % 4])
    row = (parts[0] + parts[1]) + (parts[2] + parts[3])
    rolled = pltpu.roll(jnp.broadcast_to(row[0:1], (depth, depth)), depth - half, 1, stride=1, stride_axis=0)
    w = lax.broadcasted_iota(jnp.int32, (depth, depth), 0)
    z = lax.broadcasted_iota(jnp.int32, (depth, depth), 1)
    matrix = jnp.where(jnp.abs(z - w) <= half, rolled, 0.0)
    for c in copies[6:]:
        c.wait()
    at = 0
    for table in few:
        for t in range(table.shape[0]):
            spread[at] = jnp.full((8, depth), table[t], F32)
            at += 1
    copies[1].wait()
    copies[2].wait()
    weighted = (1.0 + 3.0 * mask[...].astype(F32)) * misfit[...]
    work[...] = lax.dot_general(
        weighted, matrix, (((1,), (1,)), ((), ())),
        precision=lax.Precision.HIGHEST, preferred_element_type=F32)
    for c in copies[3:6]:
        c.wait()
    edge[...] = states[...].astype(F32).reshape(edge.shape)
    octets = nx // 8
    for y in range(ny):
        for o in range(octets):
            own[y, pl.ds(8 * o, 8), :] = work[pl.ds(8 * o * ny + y, 8, stride=ny), :]
    width = reach + RIM

    def pack(out, right):
        start = ny - width if right else 0
        for y in range(width):
            out[y] = own[start + y]
        for k in range(RIM):
            y = ny - RIM + k if right else k
            for o in range(octets):
                out[width + k, pl.ds(8 * o, 8), :] = diffusion[pl.ds(8 * o * ny + y, 8, stride=ny), :]
        y = ny - 1 if right else 0
        for o in range(octets):
            here = pl.ds(8 * o * ny + y, 8, stride=ny)
            out[width + RIM, pl.ds(8 * o, 8), :] = labels[here, :].astype(F32)
            for s in range(steps):
                at = pl.ds((s * nx + 8 * o) * ny + y, 8, stride=ny)
                out[width + RIM + 1 + s, pl.ds(8 * o, 8), :] = edge[at, :]

    def act(right):
        pack(one, right)
        pack(two, not right)

    both_ways(right_comes_first(), act)


def own_y_kernel(reach, own, spread, part):
    ny, nx, _ = own.shape
    taps = [spread[t] for t in vectors(spread, reach)[1]]
    width = (len(taps) - 1) // 2 + RIM

    @pl.loop(0, nx // 8)
    def _(o):
        at = pl.ds(pl.multiple_of(8 * o, 8), 8)

        def write(j, value):
            part[j, at, :] = value

        blur(lambda e: own[e - width, at, :], write, taps, range(ny + 2 * RIM), range(width, width + ny))


def rest_y_kernel(reach, part, one, two, labels, diffusion, states, spread, blurred, outer, inner, left, right):
    tall, nx, depth = part.shape
    ny = tall - 2 * RIM
    taps = [spread[t] for t in vectors(spread, reach)[1]]
    width = (len(taps) - 1) // 2 + RIM

    def place(first):
        left[...] = (two if first else one)[...]
        right[...] = (one if first else two)[...]

    both_ways(right_comes_first(), place)

    for o in range(nx // 8):
        at = pl.ds(8 * o, 8)

        def read(e):
            return left[e, at, :] if e < width else right[e - width - ny, at, :]

        def write(j, value):
            blurred[pl.ds(8 * o * SLOT + JOFF - RIM + j, 8, stride=SLOT), :] = value

        blur(read, write, taps, range(tall), [*range(width), *range(width + ny, 2 * width + ny)],
             base=lambda j: part[j, at, :])

    def pack(out, upper):
        at = 0
        order = range(nx - 1, -1, -1) if upper else range(nx)
        for x in order[:width]:
            out[pl.ds(at, tall), :] = blurred[pl.ds(x * SLOT + JOFF - RIM, tall), :]
            at += tall
        for x in order[:RIM]:
            for r in range(RIM):
                out[pl.ds(at + r, 1), :] = left[width + r, pl.ds(x, 1), :]
                out[pl.ds(at + RIM + ny + r, 1), :] = right[width + r, pl.ds(x, 1), :]
            out[pl.ds(at + RIM, ny), :] = diffusion[x]
            at += tall
        x = order[0]
        out[pl.ds(at, ny), :] = labels[x].astype(F32)
        at += ny
        for s in range(states.shape[0]):
            out[pl.ds(at, ny), :] = states[s, x].astype(F32)
            at += ny

    def act(even):
        pack(inner, even)
        pack(outer, not even)

    both_ways(is_even(), act)


def rate(code, table):
    return jnp.where(code == 0, table[0], jnp.where(code == 1, table[1], table[2]))


def shares(here, there):
    inverse = 1.0 / jnp.maximum(here + there, 1e-30)
    return there * inverse, here * inverse


def inside(rows, depth):
    return lax.broadcasted_iota(jnp.int32, (rows, depth), 1) < depth - 1


def early_x_kernel(reach, blurred, inner, one, two, labels, diffusion, states, spread,
                   image, coef, state, keep, cx, cy, cz, xl, xu, yl, yu, zl, zu, ext, kind):
    nx, ny, depth = labels.shape
    steps = states.shape[0]
    taps_at, _, bind_at, _ = vectors(spread, reach)
    taps = [spread[t] for t in taps_at]
    bind_t = [spread[t, 0:1, :] for t in bind_at]
    width = (len(taps) - 1) // 2 + RIM
    tall = ny + 2 * RIM
    lo, own_rows = JOFF - RIM, slice(JOFF, JOFF + ny)
    outs = range(nx + 2 * RIM)

    def place(even):
        slab = inner.at[1 if even else 0]
        at = 0
        for k in range(width):
            ext[k, lo:lo + tall, :] = slab[pl.ds(at, tall), :]
            at += tall
        first, step = (nx + RIM, 1) if even else (RIM - 1, -1)
        for k in range(RIM):
            coef[first + step * k, lo:lo + tall, :] = slab[pl.ds(at, tall), :]
            at += tall
        kind[first, own_rows, :] = slab[pl.ds(at, ny), :]
        at += ny
        for s in range(steps):
            state[s, first, own_rows, :] = slab[pl.ds(at, ny), :]
            at += ny

    both_ways(is_even(), place)

    for x in range(nx):
        p = RIM + x
        coef[p, own_rows, :] = diffusion[x]
        kind[p, own_rows, :] = labels[x].astype(F32)
        for s in range(steps):
            state[s, p, own_rows, :] = states[s, x].astype(F32)

    def rims(first):
        left, right = (two, one) if first else (one, two)
        for x in range(nx):
            p, row = RIM + x, pl.ds(x, 1)
            for k in range(RIM):
                coef[p, lo + k:lo + k + 1, :] = left[width + k, row, :]
                coef[p, JOFF + ny + k:JOFF + ny + k + 1, :] = right[width + k, row, :]
            kind[p, JOFF - 1:JOFF, :] = left[width + RIM, row, :]
            kind[p, JOFF + ny:JOFF + ny + 1, :] = right[width + RIM, row, :]
            for s in range(steps):
                state[s, p, JOFF - 1:JOFF, :] = left[width + RIM + 1 + s, row, :]
                state[s, p, JOFF + ny:JOFF + ny + 1, :] = right[width + RIM + 1 + s, row, :]

    both_ways(right_comes_first(), rims)

    @pl.loop(0, SLOT // 8)
    def _(v):
        rows = pl.ds(pl.multiple_of(8 * v, 8), 8)

        def write(i, value):
            image[i, rows, :] = value

        def near(e):
            return blurred[pl.ds(pl.multiple_of((e - width) * SLOT + 8 * v, 8), 8), :]

        blur(near, write, taps, outs, range(width, width + nx))

        def add(even):
            here = range(width + nx, 2 * width + nx) if even else range(width)
            touched = outs[nx + 2 * RIM - width:] if even else outs[:width]
            blur(lambda e: ext[e - width - nx if even else width - 1 - e, rows, :], write, taps, touched, here,
                 base=lambda i: image[i, rows, :])

        both_ways(is_even(), add)

    last = inside(SLOT, depth)

    @pl.loop(0, nx + 2 * RIM - 1, unroll=9)
    def _(p):
        h = slice(0, SLOT)
        d = coef[p, h, :]
        for there, c, low, up in ((coef[p + 1, h, :], cx, xl, xu), (coef[p, 1:SLOT + 1, :], cy, yl, yu),
                                  (pltpu.roll(d, depth - 1, 1), cz, zl, zu)):
            q, r = shares(d, there)
            if c is cz:
                q, r = jnp.where(last, q, 0.0), jnp.where(last, r, 0.0)
            c[p, h, :] = 2.0 * d * q
            low[p, h, :] = 2.0 * q * q
            up[p, h, :] = 2.0 * r * r
        keep[p, h, :] = 1.0 - 0.5 * rate(kind[p, h, :], bind_t)


def last_kernel(reach, part, coef, state, keep, cx, cy, cz, xl, xu, yl, yu, zl, zu, outer, labels, spread,
                grad_h, adjoint_h, ext, image, adj, rim, grad, adjoint, sems):
    nx, ny, depth = labels.shape
    steps = state.shape[0]
    taps_at, _, bind_at, release_at = vectors(spread, reach)
    taps = [spread[t] for t in taps_at]
    bind_t, release_t = ([spread[t, 0:1, :] for t in at] for at in (bind_at, release_at))
    width = (len(taps) - 1) // 2 + RIM
    tall = ny + 2 * RIM
    lo, own_rows = JOFF - RIM, slice(JOFF, JOFF + ny)
    outs = range(nx + 2 * RIM)
    even = is_even()

    for k in range(width):
        ext[k, lo:lo + tall, :] = outer[pl.ds(k * tall, tall), :]
    for k in range(RIM):
        rim[k, lo:lo + tall, :] = outer[pl.ds((width + k) * tall, tall), :]
    tail = (width + RIM) * tall
    rim[RIM, own_rows, :] = outer[pl.ds(tail, ny), :]
    for s in range(steps):
        rim[RIM + 1 + s, own_rows, :] = outer[pl.ds(tail + (1 + s) * ny, ny), :]

    @pl.loop(0, SLOT // 8)
    def _(v):
        rows = pl.ds(pl.multiple_of(8 * v, 8), 8)

        def write(i, value):
            image[i, rows, :] = value

        def add(even):
            far = range(width) if even else range(width + nx, 2 * width + nx)
            touched = outs[:width] if even else outs[nx + 2 * RIM - width:]
            blur(lambda e: ext[width - 1 - e if even else e - width - nx, rows, :], write, taps, touched, far,
                 base=lambda i: part[i, rows, :])
            for i in outs:
                if i not in touched:
                    image[i, rows, :] = part[i, rows, :]

        both_ways(even, add)

    h = slice(JOFF - RIM, JOFF - RIM + SLOT)
    down = slice(h.start - 1, h.stop - 1)
    after = slice(h.start + 1, h.stop + 1)

    def first(p, c_low, c_up, c_y, c_y_low, c_z, kept):
        a = image[p, h, :]
        total = c_up * (image[p + 1, h, :] - a) + c_low * (image[p - 1, h, :] - a)
        total += c_y * (image[p, after, :] - a) + c_y_low * (image[p, down, :] - a)
        fz = c_z * (pltpu.roll(a, depth - 1, 1) - a)
        adj[p, h, :] = kept * a + total + (fz - pltpu.roll(fz, 1, 1))

    def coupling(here, there):
        q, _ = shares(here, there)
        return 2.0 * here * q

    before, next_ = slice(JOFF - 1, JOFF - 1 + ny), slice(JOFF + 1, JOFF + 1 + ny)

    def second(p, c_low, s_low, state_low, c_up, s_up, state_up):
        at = own_rows
        a1, a0 = image[p, at, :], adj[p, at, :]
        s1, s0 = state[steps - 1, p, at, :], state[0, p, at, :]
        total, slopes = 0.0, 0.0

        def face(c, s, i, rows, states):
            change1, change0 = image[i, rows, :] - a1, adj[i, rows, :] - a0
            return c * change0, s * ((states[0] - s1) * change1 + (states[1] - s0) * change0)

        x = p - RIM
        for f, g in (face(c_low, s_low, p - 1, at, state_low), face(c_up, s_up, p + 1, at, state_up),
                     face(cy[p, before, :], yu[p, before, :], p, before,
                          (state[steps - 1, p, before, :], state[0, p, before, :])),
                     face(cy[p, at, :], yl[p, at, :], p, next_, (state[steps - 1, p, next_, :], state[0, p, next_, :]))):
            total, slopes = total + f, slopes + g
        nxt = functools.partial(pltpu.roll, shift=depth - 1, axis=1)
        change1, change0 = nxt(a1) - a1, nxt(a0) - a0
        both = (nxt(s1) - s1) * change1 + (nxt(s0) - s0) * change0
        fz = cz[p, at, :] * change0
        total += fz - pltpu.roll(fz, 1, 1)
        slopes += zl[p, at, :] * both + pltpu.roll(zu[p, at, :] * both, 1, 1)
        code = labels[x]
        bind, release = rate(code, bind_t), rate(code, release_t)
        b1 = 0.5 * a1 + release * (a1 - 0.5 * a1)
        grad[x] = -slopes
        adjoint[0, x] = a0 + total + bind * (b1 - a0)
        adjoint[1, x] = b1 + release * (a0 - b1)

    def send(n, x, count):
        at = pl.ds(x, count)
        pairs = ((grad.at[at], grad_h.at[at]), (adjoint.at[0, at], adjoint_h.at[0, at]),
                 (adjoint.at[1, at], adjoint_h.at[1, at]))
        return [pltpu.make_async_copy(a, b, sems.at[n, m]) for m, (a, b) in enumerate(pairs)]

    def near_rim(even):
        near, far, tile = (1, 0, RIM) if even else (nx + RIM, nx + RIM + 1, nx + RIM - 1)
        d, d_far, d_tile = rim[0, h, :], rim[1, h, :], coef[tile, h, :]
        c_tile, c_far = coupling(d, d_tile), coupling(d, d_far)
        c_z = jnp.where(inside(SLOT, depth), coupling(d, pltpu.roll(d, depth - 1, 1)), 0.0)
        kept = 1.0 - 0.5 * rate(rim[RIM, h, :], bind_t)
        c_low, c_up = (c_far, c_tile) if even else (c_tile, c_far)
        first(near, c_low, c_up, coupling(d, rim[0, after, :]), coupling(d, rim[0, down, :]), c_z, kept)
        inner_face = cx[tile, h, :] if even else cx[tile - 1, h, :]
        c_low, c_up = (c_tile, inner_face) if even else (inner_face, c_tile)
        first(tile, c_low, c_up, cy[tile, h, :], cy[tile, down, :], cz[tile, h, :], keep[tile, h, :])

    def near_rim_second(even):
        tile = RIM if even else nx + RIM - 1
        at = own_rows
        q, r = shares(coef[tile, at, :], rim[0, at, :])
        far = (2.0 * coef[tile, at, :] * q, 2.0 * q * q, (rim[RIM + steps, at, :], rim[RIM + 1, at, :]))
        if even:
            second(tile, *far, cx[tile, at, :], xl[tile, at, :],
                   (state[steps - 1, tile + 1, at, :], state[0, tile + 1, at, :]))
        else:
            second(tile, cx[tile - 1, at, :], xu[tile - 1, at, :],
                   (state[steps - 1, tile - 1, at, :], state[0, tile - 1, at, :]), *far)

    both_ways(even, near_rim)

    @pl.loop(0, nx, unroll=8)
    def _(n):
        p = n + jnp.where(even, RIM + 1, 1)
        first(p, cx[p - 1, h, :], cx[p, h, :], cy[p, h, :], cy[p, down, :], cz[p, h, :], keep[p, h, :])

    both_ways(even, near_rim_second)
    copies = send(0, jnp.where(even, 0, nx - 1), 1)
    for c in copies:
        c.start()
    base = jnp.where(even, RIM + 1, RIM)
    size = -(-(nx - 1) // CHUNKS)
    for n in range(CHUNKS):
        count = min(size, nx - 1 - n * size)

        @pl.loop(n * size, n * size + count, unroll=count)
        def _(k):
            p = base + k
            at = own_rows
            second(p, cx[p - 1, at, :], xu[p - 1, at, :], (state[steps - 1, p - 1, at, :], state[0, p - 1, at, :]),
                   cx[p, at, :], xl[p, at, :], (state[steps - 1, p + 1, at, :], state[0, p + 1, at, :]))

        more = send(n + 1, base - RIM + n * size, count)
        for c in more:
            c.start()
        copies += more
    for c in copies:
        c.wait()


def swap_along_gy(shape, parity):
    nx, ny = shape
    pairs = []
    for i in range(nx):
        for j in range((parity + i + 1) % 2, ny - 1, 2):
            a, b = i * ny + j, i * ny + j + 1
            pairs += [(a, b), (b, a)]
    return pairs


def shards(misfit, bleach_mask, labels, diffusion, bind_table, release_table, kern_x, kern_y, kern_z, free_states):
    nx, ny, depth = misfit.shape
    steps = free_states.shape[0]
    reach = (kern_x.shape[0] - 1) // 2
    width = reach + RIM
    tall = ny + 2 * RIM
    shape = (lax.axis_size("gx"), lax.axis_size("gy"))
    vmem = pl.BlockSpec(memory_space=pltpu.VMEM)
    hbm = pl.BlockSpec(memory_space=pl.ANY)
    params = pltpu.CompilerParams(vmem_limit_bytes=24 * 1024 * 1024)
    flat = (nx * ny, depth)
    array = jax.ShapeDtypeStruct

    def in_hbm(x):
        return pltpu.with_memory_space_constraint(x, pltpu.MemorySpace.HBM)

    slots = width + RIM + 1 + steps
    slab = array((slots, nx, depth), F32)
    few = (kern_x, kern_y, bind_table, release_table)
    own, one, two, spread = pl.pallas_call(
        functools.partial(first_kernel, reach),
        out_shape=[array((ny, nx, depth), F32), slab, slab, array((sum(t.shape[0] for t in few), 8, depth), F32)],
        in_specs=[hbm] * (6 + len(few)),
        out_specs=[vmem] * 4,
        scratch_shapes=[
            pltpu.VMEM(flat, F32), pltpu.VMEM(flat, jnp.int32), pltpu.VMEM(flat, jnp.int32), pltpu.VMEM(flat, F32),
            pltpu.VMEM(free_states.shape, free_states.dtype), pltpu.SMEM(kern_z.shape, F32),
            pltpu.VMEM(flat, F32), pltpu.VMEM((steps * nx * ny, depth), F32),
            *(pltpu.SMEM(t.shape, F32) for t in few), pltpu.SemaphoreType.DMA((6 + len(few),))],
        compiler_params=params,
        name="weigh_blur_z",
    )(in_hbm(misfit.reshape(flat)), in_hbm(bleach_mask.reshape(flat)), in_hbm(labels.reshape(flat)),
      in_hbm(diffusion.reshape(flat)), in_hbm(free_states), in_hbm(kern_z), *map(in_hbm, few))
    one = lax.ppermute(one, AXES, swap_along_gy(shape, 0))
    two = lax.ppermute(two, AXES, swap_along_gy(shape, 1))

    part = pl.pallas_call(
        functools.partial(own_y_kernel, reach),
        out_shape=array((tall, nx, depth), F32),
        in_specs=[vmem] * 2,
        out_specs=vmem,
        compiler_params=params,
        cost_estimate=pl.CostEstimate(flops=4_000_000, bytes_accessed=700_000, transcendentals=0),
        name="own_y",
    )(own, spread)

    rows = (width + RIM) * tall + (1 + steps) * ny
    slab = array((rows, depth), F32)
    blurred, outer, inner = pl.pallas_call(
        functools.partial(rest_y_kernel, reach),
        out_shape=[array((nx * SLOT, depth), F32), slab, slab],
        in_specs=[vmem] * 7,
        out_specs=[vmem] * 3,
        scratch_shapes=[pltpu.VMEM((slots, nx, depth), F32)] * 2,
        compiler_params=params,
        name="rest_y",
    )(part, one, two, labels, diffusion, free_states, spread)

    line = shape[1]
    across = []
    for i in range(1, shape[0] - 1, 2):
        for j in range(line):
            a, b = i * line + j, (i + 1) * line + j
            across += [(a, b), (b, a)]
    within = [[i * line + j, (i + 1) * line + j] for i in range(0, shape[0], 2) for j in range(line)]
    outer = lax.ppermute(outer, AXES, across)
    inner = lax.all_gather(inner, AXES, axis_index_groups=within)

    around = (nx + 2 * RIM, HIGH, depth)
    field = array(around, F32)
    early = pl.pallas_call(
        functools.partial(early_x_kernel, reach),
        out_shape=[field, field, array((steps, *around), F32)] + [field] * 10,
        in_specs=[vmem] * 8,
        out_specs=[vmem] * 13,
        scratch_shapes=[pltpu.VMEM((width, SLOT, depth), F32), pltpu.VMEM(around, F32)],
        compiler_params=params,
        cost_estimate=pl.CostEstimate(flops=8_000_000, bytes_accessed=3_000_000, transcendentals=0),
        name="early_x",
    )(blurred, inner, one, two, labels, diffusion, free_states, spread)

    tile = (nx, ny, depth)
    grad, adjoint = pl.pallas_call(
        functools.partial(last_kernel, reach),
        out_shape=[array(tile, F32), array((2, *tile), F32)],
        in_specs=[vmem] * 16,
        out_specs=[hbm] * 2,
        scratch_shapes=[
            pltpu.VMEM((width, SLOT, depth), F32),
            pltpu.VMEM(around, F32),
            pltpu.VMEM(around, F32),
            pltpu.VMEM((RIM + 1 + steps, HIGH, depth), F32),
            pltpu.VMEM(tile, F32),
            pltpu.VMEM((2, *tile), F32),
            pltpu.SemaphoreType.DMA((CHUNKS + 1, 3)),
        ],
        compiler_params=params,
        name="late_x_steps",
    )(*early, outer, labels, spread)
    return grad, adjoint


def solution(mesh):
    tile = P("gx", "gy", None)
    in_specs = (tile, tile, tile, tile, P(), P(), P(), P(), P(), P(None, "gx", "gy", None))
    out_specs = (tile, P(None, "gx", "gy", None))
    return jax.shard_map(shards, mesh=mesh, in_specs=in_specs, out_specs=out_specs, check_vma=False)
```

```python
import functools

import jax
import jax.numpy as jnp
from jax import lax
from jax.experimental import pallas as pl
from jax.experimental.pallas import tpu as pltpu
from jax.sharding import PartitionSpec as P

AXES = ("gx", "gy")
RIM = 2
JOFF = 4
SLOT = 32
HIGH = 40
CHUNKS = 4
F32 = jnp.float32
STEP_ROWS = tuple(slice(JOFF - RIM + k, JOFF - RIM + k + SLOT) for k in (0, -1, 1))


def blur(read, write, taps, outs, sources, group=14, base=None):
    span = len(taps)
    for start in range(0, len(outs), group):
        mine = outs[start:start + group]
        acc = {i: base(i) for i in mine} if base else {}
        for e in sources:
            users = [i for i in mine if 0 <= e - i < span]
            if users:
                value = read(e)
            for i in users:
                term = taps[e - i] * value
                acc[i] = acc[i] + term if i in acc else term
        for i in mine:
            write(i, acc[i])


def vectors(spread, reach):
    span = 2 * reach + 1
    taps_x, taps_y, bind = range(span), range(span, 2 * span), 2 * span
    kinds = (spread.shape[0] - bind) // 2
    return taps_x, taps_y, range(bind, bind + kinds), range(bind + kinds, bind + 2 * kinds)


def right_comes_first():
    return (lax.axis_index("gx") + lax.axis_index("gy")) % 2 == 1


def is_even():
    return lax.axis_index("gx") % 2 == 0


def both_ways(flag, act):
    pl.when(flag)(functools.partial(act, True))
    pl.when(jnp.logical_not(flag))(functools.partial(act, False))


def first_kernel(reach, misfit_h, mask_h, labels_h, diffusion_h, states_h, kern_h, *rest):
    few_h, rest = rest[:4], rest[4:]
    own, one, two, spread, labels, diffusion, states, misfit, mask, kern, work, edge, *few, sems = rest
    steps, nx, ny, depth = states.shape
    copies = [pltpu.make_async_copy(a, b, sems.at[n]) for n, (a, b) in enumerate(
        ((kern_h, kern), (misfit_h, misfit), (mask_h, mask), (diffusion_h, diffusion), (labels_h, labels), (states_h, states), *zip(few_h, few)))]
    for c in copies[:3] + copies[6:] + copies[3:6]:
        c.start()
    taps_z = kern.shape[0]
    half = (taps_z - 1) // 2
    copies[0].wait()
    lane = lax.broadcasted_iota(jnp.int32, (8, depth), 1)
    parts = [jnp.zeros((8, depth), F32) for _ in range(4)]
    for t in range(taps_z):
        parts[t % 4] = jnp.where(lane == t, kern[t], parts[t % 4])
    row = (parts[0] + parts[1]) + (parts[2] + parts[3])
    rolled = pltpu.roll(jnp.broadcast_to(row[0:1], (depth, depth)), depth - half, 1, stride=1, stride_axis=0)
    w = lax.broadcasted_iota(jnp.int32, (depth, depth), 0)
    z = lax.broadcasted_iota(jnp.int32, (depth, depth), 1)
    matrix = jnp.where(jnp.abs(z - w) <= half, rolled, 0.0)
    for c in copies[6:]:
        c.wait()
    at = 0
    for table in few:
        for t in range(table.shape[0]):
            spread[at] = jnp.full((8, depth), table[t], F32)
            at += 1
    copies[1].wait()
    copies[2].wait()
    weighted = (1.0 + 3.0 * mask[...].astype(F32)) * misfit[...]
    work[...] = lax.dot_general(
        weighted, matrix, (((1,), (1,)), ((), ())),
        precision=lax.Precision.HIGHEST, preferred_element_type=F32)
    for c in copies[3:6]:
        c.wait()
    edge[...] = states[...].astype(F32).reshape(edge.shape)
    octets = nx // 8
    for y in range(ny):
        for o in range(octets):
            own[y, pl.ds(8 * o, 8), :] = work[pl.ds(8 * o * ny + y, 8, stride=ny), :]
    width = reach + RIM

    def pack(out, right):
        start = ny - width if right else 0
        for y in range(width):
            out[y] = own[start + y]
        for k in range(RIM):
            y = ny - RIM + k if right else k
            for o in range(octets):
                out[width + k, pl.ds(8 * o, 8), :] = diffusion[pl.ds(8 * o * ny + y, 8, stride=ny), :]
        y = ny - 1 if right else 0
        for o in range(octets):
            here = pl.ds(8 * o * ny + y, 8, stride=ny)
            out[width + RIM, pl.ds(8 * o, 8), :] = labels[here, :].astype(F32)
            for s in range(steps):
                at = pl.ds((s * nx + 8 * o) * ny + y, 8, stride=ny)
                out[width + RIM + 1 + s, pl.ds(8 * o, 8), :] = edge[at, :]

    def act(right):
        pack(one, right)
        pack(two, not right)

    both_ways(right_comes_first(), act)


def own_y_kernel(reach, own, spread, part):
    ny, nx, _ = own.shape
    taps = [spread[t] for t in vectors(spread, reach)[1]]
    width = (len(taps) - 1) // 2 + RIM

    @pl.loop(0, nx // 8)
    def _(o):
        at = pl.ds(pl.multiple_of(8 * o, 8), 8)

        def write(j, value):
            part[j, at, :] = value

        blur(lambda e: own[e - width, at, :], write, taps, range(ny + 2 * RIM), range(width, width + ny))


def rest_y_kernel(reach, part, one, two, labels, diffusion, states, spread, blurred, outer, inner, left, right):
    tall, nx, depth = part.shape
    ny = tall - 2 * RIM
    taps = [spread[t] for t in vectors(spread, reach)[1]]
    width = (len(taps) - 1) // 2 + RIM

    def place(first):
        left[...] = (two if first else one)[...]
        right[...] = (one if first else two)[...]

    both_ways(right_comes_first(), place)

    for o in range(nx // 8):
        at = pl.ds(8 * o, 8)

        def read(e):
            return left[e, at, :] if e < width else right[e - width - ny, at, :]

        def write(j, value):
            blurred[pl.ds(8 * o * SLOT + JOFF - RIM + j, 8, stride=SLOT), :] = value

        blur(read, write, taps, range(tall), [*range(width), *range(width + ny, 2 * width + ny)],
             base=lambda j: part[j, at, :])

    def pack(out, upper):
        at = 0
        order = range(nx - 1, -1, -1) if upper else range(nx)
        for x in order[:width]:
            out[pl.ds(at, tall), :] = blurred[pl.ds(x * SLOT + JOFF - RIM, tall), :]
            at += tall
        for x in order[:RIM]:
            for r in range(RIM):
                out[pl.ds(at + r, 1), :] = left[width + r, pl.ds(x, 1), :]
                out[pl.ds(at + RIM + ny + r, 1), :] = right[width + r, pl.ds(x, 1), :]
            out[pl.ds(at + RIM, ny), :] = diffusion[x]
            at += tall
        x = order[0]
        out[pl.ds(at, ny), :] = labels[x].astype(F32)
        at += ny
        for s in range(states.shape[0]):
            out[pl.ds(at, ny), :] = states[s, x].astype(F32)
            at += ny

    def act(even):
        pack(inner, even)
        pack(outer, not even)

    both_ways(is_even(), act)


def rate(code, table):
    return jnp.where(code == 0, table[0], jnp.where(code == 1, table[1], table[2]))


def shares(here, there):
    inverse = 1.0 / jnp.maximum(here + there, 1e-30)
    return there * inverse, here * inverse


def inside(rows, depth):
    return lax.broadcasted_iota(jnp.int32, (rows, depth), 1) < depth - 1


def stepper(image, adj, coef, state, keep, cx, cy, cz, xl, xu, yl, yu, zl, zu, labels, bind_t, release_t, put):
    steps, ny, depth = state.shape[0], labels.shape[1], labels.shape[2]
    h, down, after = STEP_ROWS
    own_rows = slice(JOFF, JOFF + ny)
    before, next_ = slice(JOFF - 1, JOFF - 1 + ny), slice(JOFF + 1, JOFF + 1 + ny)

    def first(p, c_low, c_up, c_y, c_y_low, c_z, kept):
        a = image[p, h, :]
        total = c_up * (image[p + 1, h, :] - a) + c_low * (image[p - 1, h, :] - a)
        total += c_y * (image[p, after, :] - a) + c_y_low * (image[p, down, :] - a)
        fz = c_z * (pltpu.roll(a, depth - 1, 1) - a)
        adj[p, h, :] = kept * a + total + (fz - pltpu.roll(fz, 1, 1))

    def first_plain(p):
        first(p, cx[p - 1, h, :], cx[p, h, :], cy[p, h, :], cy[p, down, :], cz[p, h, :], keep[p, h, :])

    def second(p, c_low, s_low, state_low, c_up, s_up, state_up):
        at = own_rows
        a1, a0 = image[p, at, :], adj[p, at, :]
        s1, s0 = state[steps - 1, p, at, :], state[0, p, at, :]
        total, slopes = 0.0, 0.0

        def face(c, s, i, rows, states):
            change1, change0 = image[i, rows, :] - a1, adj[i, rows, :] - a0
            return c * change0, s * ((states[0] - s1) * change1 + (states[1] - s0) * change0)

        x = p - RIM
        for f, g in (face(c_low, s_low, p - 1, at, state_low), face(c_up, s_up, p + 1, at, state_up),
                     face(cy[p, before, :], yu[p, before, :], p, before,
                          (state[steps - 1, p, before, :], state[0, p, before, :])),
                     face(cy[p, at, :], yl[p, at, :], p, next_, (state[steps - 1, p, next_, :], state[0, p, next_, :]))):
            total, slopes = total + f, slopes + g
        nxt = functools.partial(pltpu.roll, shift=depth - 1, axis=1)
        change1, change0 = nxt(a1) - a1, nxt(a0) - a0
        both = (nxt(s1) - s1) * change1 + (nxt(s0) - s0) * change0
        fz = cz[p, at, :] * change0
        total += fz - pltpu.roll(fz, 1, 1)
        slopes += zl[p, at, :] * both + pltpu.roll(zu[p, at, :] * both, 1, 1)
        code = labels[x]
        bind, release = rate(code, bind_t), rate(code, release_t)
        b1 = 0.5 * a1 + release * (a1 - 0.5 * a1)
        put(x, -slopes, a0 + total + bind * (b1 - a0), b1 + release * (a0 - b1))

    def second_plain(p):
        at = own_rows
        second(p, cx[p - 1, at, :], xu[p - 1, at, :], (state[steps - 1, p - 1, at, :], state[0, p - 1, at, :]),
               cx[p, at, :], xl[p, at, :], (state[steps - 1, p + 1, at, :], state[0, p + 1, at, :]))

    return first, first_plain, second, second_plain


def free_slots(nx, width, even):
    return jnp.where(even, width + RIM, RIM), nx - width


def early_x_kernel(reach, blurred, inner, one, two, labels, diffusion, states, spread,
                   image, coef, state, keep, cx, cy, cz, xl, xu, yl, yu, zl, zu, done_adj, done, ext, kind, adj):
    nx, ny, depth = labels.shape
    steps = states.shape[0]
    taps_at, _, bind_at, release_at = vectors(spread, reach)
    taps = [spread[t] for t in taps_at]
    bind_t, release_t = ([spread[t, 0:1, :] for t in at] for at in (bind_at, release_at))
    width = (len(taps) - 1) // 2 + RIM
    tall = ny + 2 * RIM
    lo, own_rows = JOFF - RIM, slice(JOFF, JOFF + ny)
    outs = range(nx + 2 * RIM)

    def place(even):
        slab = inner.at[1 if even else 0]
        at = 0
        for k in range(width):
            ext[k, lo:lo + tall, :] = slab[pl.ds(at, tall), :]
            at += tall
        first, step = (nx + RIM, 1) if even else (RIM - 1, -1)
        for k in range(RIM):
            coef[first + step * k, lo:lo + tall, :] = slab[pl.ds(at, tall), :]
            at += tall
        kind[first, own_rows, :] = slab[pl.ds(at, ny), :]
        at += ny
        for s in range(steps):
            state[s, first, own_rows, :] = slab[pl.ds(at, ny), :]
            at += ny

    both_ways(is_even(), place)

    for x in range(nx):
        p = RIM + x
        coef[p, own_rows, :] = diffusion[x]
        kind[p, own_rows, :] = labels[x].astype(F32)
        for s in range(steps):
            state[s, p, own_rows, :] = states[s, x].astype(F32)

    def rims(first):
        left, right = (two, one) if first else (one, two)
        for x in range(nx):
            p, row = RIM + x, pl.ds(x, 1)
            for k in range(RIM):
                coef[p, lo + k:lo + k + 1, :] = left[width + k, row, :]
                coef[p, JOFF + ny + k:JOFF + ny + k + 1, :] = right[width + k, row, :]
            kind[p, JOFF - 1:JOFF, :] = left[width + RIM, row, :]
            kind[p, JOFF + ny:JOFF + ny + 1, :] = right[width + RIM, row, :]
            for s in range(steps):
                state[s, p, JOFF - 1:JOFF, :] = left[width + RIM + 1 + s, row, :]
                state[s, p, JOFF + ny:JOFF + ny + 1, :] = right[width + RIM + 1 + s, row, :]

    both_ways(right_comes_first(), rims)

    @pl.loop(0, SLOT // 8)
    def _(v):
        rows = pl.ds(pl.multiple_of(8 * v, 8), 8)

        def write(i, value):
            image[i, rows, :] = value

        def near(e):
            return blurred[pl.ds(pl.multiple_of((e - width) * SLOT + 8 * v, 8), 8), :]

        blur(near, write, taps, outs, range(width, width + nx))

        def add(even):
            here = range(width + nx, 2 * width + nx) if even else range(width)
            touched = outs[nx + 2 * RIM - width:] if even else outs[:width]
            blur(lambda e: ext[e - width - nx if even else width - 1 - e, rows, :], write, taps, touched, here,
                 base=lambda i: image[i, rows, :])

        both_ways(is_even(), add)

    last = inside(SLOT, depth)

    @pl.loop(0, nx + 2 * RIM - 1, unroll=9)
    def _(p):
        h = slice(0, SLOT)
        d = coef[p, h, :]
        for there, c, low, up in ((coef[p + 1, h, :], cx, xl, xu), (coef[p, 1:SLOT + 1, :], cy, yl, yu),
                                  (pltpu.roll(d, depth - 1, 1), cz, zl, zu)):
            q, r = shares(d, there)
            if c is cz:
                q, r = jnp.where(last, q, 0.0), jnp.where(last, r, 0.0)
            c[p, h, :] = 2.0 * d * q
            low[p, h, :] = 2.0 * q * q
            up[p, h, :] = 2.0 * r * r
        keep[p, h, :] = 1.0 - 0.5 * rate(kind[p, h, :], bind_t)

    even = is_even()
    lower, count = free_slots(nx, width, even)

    def put(x, *results):
        for n, value in enumerate(results):
            done[n, x + RIM - lower] = value

    _, first, _, second = stepper(image, adj, coef, state, keep, cx, cy, cz, xl, xu, yl, yu, zl, zu, labels, bind_t, release_t, put)

    @pl.loop(0, count + 2, unroll=count + 2)
    def _(n):
        first(lower - 1 + n)

    @pl.loop(0, count, unroll=count)
    def _(n):
        second(lower + n)

    def keep_nearest(even):
        for n in range(2):
            done_adj[n] = adj[width + 1 + n if even else nx + 2 * RIM - 2 - width - n]

    both_ways(even, keep_nearest)


def last_kernel(reach, part, coef, state, keep, cx, cy, cz, xl, xu, yl, yu, zl, zu, outer, labels, spread,
                done_adj, done, grad_h, adjoint_h, ext, image, adj, rim, grad, adjoint, sems):
    nx, ny, depth = labels.shape
    steps = state.shape[0]
    taps_at, _, bind_at, release_at = vectors(spread, reach)
    taps = [spread[t] for t in taps_at]
    bind_t, release_t = ([spread[t, 0:1, :] for t in at] for at in (bind_at, release_at))
    width = (len(taps) - 1) // 2 + RIM
    tall = ny + 2 * RIM
    lo, own_rows = JOFF - RIM, slice(JOFF, JOFF + ny)
    outs = range(nx + 2 * RIM)
    even = is_even()

    lower, count = free_slots(nx, width, even)
    at = pl.ds(lower - RIM, count)
    copies = [pltpu.make_async_copy(done.at[n], target, sems.at[CHUNKS + 1, n])
              for n, target in enumerate((grad_h.at[at], adjoint_h.at[0, at], adjoint_h.at[1, at]))]
    for c in copies:
        c.start()

    for k in range(width):
        ext[k, lo:lo + tall, :] = outer[pl.ds(k * tall, tall), :]
    for k in range(RIM):
        rim[k, lo:lo + tall, :] = outer[pl.ds((width + k) * tall, tall), :]
    tail = (width + RIM) * tall
    rim[RIM, own_rows, :] = outer[pl.ds(tail, ny), :]
    for s in range(steps):
        rim[RIM + 1 + s, own_rows, :] = outer[pl.ds(tail + (1 + s) * ny, ny), :]

    @pl.loop(0, SLOT // 8)
    def _(v):
        rows = pl.ds(pl.multiple_of(8 * v, 8), 8)

        def write(i, value):
            image[i, rows, :] = value

        def add(even):
            far = range(width) if even else range(width + nx, 2 * width + nx)
            touched = outs[:width] if even else outs[nx + 2 * RIM - width:]
            blur(lambda e: ext[width - 1 - e if even else e - width - nx, rows, :], write, taps, touched, far,
                 base=lambda i: part[i, rows, :])
            for i in outs:
                if i not in touched:
                    image[i, rows, :] = part[i, rows, :]

        both_ways(even, add)

    def put(x, *results):
        grad[x], adjoint[0, x], adjoint[1, x] = results

    first, first_plain, second, second_plain = stepper(
        image, adj, coef, state, keep, cx, cy, cz, xl, xu, yl, yu, zl, zu, labels, bind_t, release_t, put)
    h, down, after = STEP_ROWS

    def coupling(here, there):
        q, _ = shares(here, there)
        return 2.0 * here * q

    def send(n, x, count):
        at = pl.ds(x, count)
        pairs = ((grad.at[at], grad_h.at[at]), (adjoint.at[0, at], adjoint_h.at[0, at]),
                 (adjoint.at[1, at], adjoint_h.at[1, at]))
        return [pltpu.make_async_copy(a, b, sems.at[n, m]) for m, (a, b) in enumerate(pairs)]

    def near_rim(even):
        near, far, tile = (1, 0, RIM) if even else (nx + RIM, nx + RIM + 1, nx + RIM - 1)
        d, d_far, d_tile = rim[0, h, :], rim[1, h, :], coef[tile, h, :]
        c_tile, c_far = coupling(d, d_tile), coupling(d, d_far)
        c_z = jnp.where(inside(SLOT, depth), coupling(d, pltpu.roll(d, depth - 1, 1)), 0.0)
        kept = 1.0 - 0.5 * rate(rim[RIM, h, :], bind_t)
        c_low, c_up = (c_far, c_tile) if even else (c_tile, c_far)
        first(near, c_low, c_up, coupling(d, rim[0, after, :]), coupling(d, rim[0, down, :]), c_z, kept)
        inner_face = cx[tile, h, :] if even else cx[tile - 1, h, :]
        c_low, c_up = (c_tile, inner_face) if even else (inner_face, c_tile)
        first(tile, c_low, c_up, cy[tile, h, :], cy[tile, down, :], cz[tile, h, :], keep[tile, h, :])

    def near_rim_second(even):
        tile = RIM if even else nx + RIM - 1
        at = own_rows
        q, r = shares(coef[tile, at, :], rim[0, at, :])
        far = (2.0 * coef[tile, at, :] * q, 2.0 * q * q, (rim[RIM + steps, at, :], rim[RIM + 1, at, :]))
        if even:
            second(tile, *far, cx[tile, at, :], xl[tile, at, :],
                   (state[steps - 1, tile + 1, at, :], state[0, tile + 1, at, :]))
        else:
            second(tile, cx[tile - 1, at, :], xu[tile - 1, at, :],
                   (state[steps - 1, tile - 1, at, :], state[0, tile - 1, at, :]), *far)

    both_ways(even, near_rim)

    def take(even):
        for n in range(2):
            adj[width + 1 + n if even else nx + 2 * RIM - 2 - width - n] = done_adj[n]

    both_ways(even, take)
    left = width - RIM
    low = jnp.where(even, RIM + 1, nx + 1 - left)

    @pl.loop(0, left, unroll=5)
    def _(n):
        first_plain(low + n)

    both_ways(even, near_rim_second)
    more = send(0, jnp.where(even, 0, nx - 1), 1)
    for c in more:
        c.start()
    copies += more
    base = jnp.where(even, RIM + 1, nx - left)
    size = (left + 1) // CHUNKS

    @pl.loop(0, CHUNKS)
    def _(n):
        for k in range(size):
            second_plain(base + n * size + k)
        for c in send(n + 1, base - RIM + n * size, size):
            c.start()

    for n in range(CHUNKS):
        copies += send(n + 1, base - RIM + n * size, size)
    for c in copies:
        c.wait()


def swap_along_gy(shape, parity):
    nx, ny = shape
    pairs = []
    for i in range(nx):
        for j in range((parity + i + 1) % 2, ny - 1, 2):
            a, b = i * ny + j, i * ny + j + 1
            pairs += [(a, b), (b, a)]
    return pairs


def shards(misfit, bleach_mask, labels, diffusion, bind_table, release_table, kern_x, kern_y, kern_z, free_states):
    nx, ny, depth = misfit.shape
    steps = free_states.shape[0]
    reach = (kern_x.shape[0] - 1) // 2
    width = reach + RIM
    tall = ny + 2 * RIM
    shape = (lax.axis_size("gx"), lax.axis_size("gy"))
    vmem = pl.BlockSpec(memory_space=pltpu.VMEM)
    hbm = pl.BlockSpec(memory_space=pl.ANY)
    params = pltpu.CompilerParams(vmem_limit_bytes=24 * 1024 * 1024)
    flat = (nx * ny, depth)
    array = jax.ShapeDtypeStruct

    def in_hbm(x):
        return pltpu.with_memory_space_constraint(x, pltpu.MemorySpace.HBM)

    slots = width + RIM + 1 + steps
    slab = array((slots, nx, depth), F32)
    few = (kern_x, kern_y, bind_table, release_table)
    own, one, two, spread, held_labels, held_diffusion, held_states = pl.pallas_call(
        functools.partial(first_kernel, reach),
        out_shape=[array((ny, nx, depth), F32), slab, slab, array((sum(t.shape[0] for t in few), 8, depth), F32),
                   array(flat, jnp.int32), array(flat, F32), array(free_states.shape, free_states.dtype)],
        in_specs=[hbm] * (6 + len(few)),
        out_specs=[vmem] * 7,
        scratch_shapes=[
            pltpu.VMEM(flat, F32), pltpu.VMEM(flat, jnp.int32), pltpu.SMEM(kern_z.shape, F32),
            pltpu.VMEM(flat, F32), pltpu.VMEM((steps * nx * ny, depth), F32),
            *(pltpu.SMEM(t.shape, F32) for t in few), pltpu.SemaphoreType.DMA((6 + len(few),))],
        compiler_params=params,
        name="weigh_blur_z",
    )(in_hbm(misfit.reshape(flat)), in_hbm(bleach_mask.reshape(flat)), in_hbm(labels.reshape(flat)),
      in_hbm(diffusion.reshape(flat)), in_hbm(free_states), in_hbm(kern_z), *map(in_hbm, few))
    labels, diffusion = held_labels.reshape(labels.shape), held_diffusion.reshape(diffusion.shape)
    one = lax.ppermute(one, AXES, swap_along_gy(shape, 0))
    two = lax.ppermute(two, AXES, swap_along_gy(shape, 1))

    part = pl.pallas_call(
        functools.partial(own_y_kernel, reach),
        out_shape=array((tall, nx, depth), F32),
        in_specs=[vmem] * 2,
        out_specs=vmem,
        compiler_params=params,
        cost_estimate=pl.CostEstimate(flops=4_000_000, bytes_accessed=700_000, transcendentals=0),
        name="own_y",
    )(own, spread)

    rows = (width + RIM) * tall + (1 + steps) * ny
    slab = array((rows, depth), F32)
    blurred, outer, inner = pl.pallas_call(
        functools.partial(rest_y_kernel, reach),
        out_shape=[array((nx * SLOT, depth), F32), slab, slab],
        in_specs=[vmem] * 7,
        out_specs=[vmem] * 3,
        scratch_shapes=[pltpu.VMEM((slots, nx, depth), F32)] * 2,
        compiler_params=params,
        name="rest_y",
    )(part, one, two, labels, diffusion, held_states, spread)

    line = shape[1]
    across = []
    for i in range(1, shape[0] - 1, 2):
        for j in range(line):
            a, b = i * line + j, (i + 1) * line + j
            across += [(a, b), (b, a)]
    within = [[i * line + j, (i + 1) * line + j] for i in range(0, shape[0], 2) for j in range(line)]
    outer = lax.ppermute(outer, AXES, across)
    inner = lax.all_gather(inner, AXES, axis_index_groups=within)

    around = (nx + 2 * RIM, HIGH, depth)
    field = array(around, F32)
    *early, done_adj, done = pl.pallas_call(
        functools.partial(early_x_kernel, reach),
        out_shape=[field, field, array((steps, *around), F32)] + [field] * 10
        + [array((2, *around[1:]), F32), array((3, nx - width, ny, depth), F32)],
        in_specs=[vmem] * 8,
        out_specs=[vmem] * 15,
        scratch_shapes=[pltpu.VMEM((width, SLOT, depth), F32), pltpu.VMEM(around, F32), pltpu.VMEM(around, F32)],
        compiler_params=params,
        cost_estimate=pl.CostEstimate(flops=8_000_000, bytes_accessed=3_000_000, transcendentals=0),
        name="early_x",
    )(blurred, inner, one, two, labels, diffusion, held_states, spread)

    tile = (nx, ny, depth)
    grad, adjoint = pl.pallas_call(
        functools.partial(last_kernel, reach),
        out_shape=[array(tile, F32), array((2, *tile), F32)],
        in_specs=[vmem] * 18,
        out_specs=[hbm] * 2,
        scratch_shapes=[
            pltpu.VMEM((width, SLOT, depth), F32),
            pltpu.VMEM(around, F32),
            pltpu.VMEM(around, F32),
            pltpu.VMEM((RIM + 1 + steps, HIGH, depth), F32),
            pltpu.VMEM(tile, F32),
            pltpu.VMEM((2, *tile), F32),
            pltpu.SemaphoreType.DMA((CHUNKS + 2, 3)),
        ],
        compiler_params=params,
        name="late_x_steps",
    )(*early, outer, labels, spread, done_adj, done)
    return grad, adjoint


def solution(mesh):
    tile = P("gx", "gy", None)
    in_specs = (tile, tile, tile, tile, P(), P(), P(), P(), P(), P(None, "gx", "gy", None))
    out_specs = (tile, P(None, "gx", "gy", None))
    return jax.shard_map(shards, mesh=mesh, in_specs=in_specs, out_specs=out_specs, check_vma=False)
```

```python
import functools

import jax
import jax.numpy as jnp
from jax import lax
from jax.experimental import pallas as pl
from jax.experimental.pallas import tpu as pltpu
from jax.sharding import PartitionSpec as P

AXES = ("gx", "gy")
RIM = 2
JOFF = 4
SLOT = 32
HIGH = 40
CHUNKS = 2
F32 = jnp.float32
STEP_ROWS = tuple(slice(JOFF - RIM + k, JOFF - RIM + k + SLOT) for k in (0, -1, 1))


def blur(read, write, taps, outs, sources, group=14, base=None):
    span = len(taps)
    for start in range(0, len(outs), group):
        mine = outs[start:start + group]
        acc = {i: base(i) for i in mine} if base else {}
        for e in sources:
            users = [i for i in mine if 0 <= e - i < span]
            if users:
                value = read(e)
            for i in users:
                term = taps[e - i] * value
                acc[i] = acc[i] + term if i in acc else term
        for i in mine:
            write(i, acc[i])


def vectors(spread, reach):
    span = 2 * reach + 1
    taps_x, taps_y, bind = range(span), range(span, 2 * span), 2 * span
    kinds = (spread.shape[0] - bind) // 2
    return taps_x, taps_y, range(bind, bind + kinds), range(bind + kinds, bind + 2 * kinds)


def right_comes_first():
    return (lax.axis_index("gx") + lax.axis_index("gx") // 2 + lax.axis_index("gy")) % 2 == 1


def is_even():
    return lax.axis_index("gx") % 2 == 0


def both_ways(flag, act):
    pl.when(flag)(functools.partial(act, True))
    pl.when(jnp.logical_not(flag))(functools.partial(act, False))


def first_kernel(reach, misfit_h, mask_h, labels_h, diffusion_h, states_h, kern_h, *rest):
    few_h, rest = rest[:4], rest[4:]
    own, one, two, spread, labels, diffusion, states, misfit, mask, kern, work, edge, *few, sems = rest
    steps, nx, ny, depth = states.shape
    copies = [pltpu.make_async_copy(a, b, sems.at[n]) for n, (a, b) in enumerate(
        ((kern_h, kern), (misfit_h, misfit), (mask_h, mask), (diffusion_h, diffusion), (labels_h, labels), (states_h, states), *zip(few_h, few)))]
    for c in copies[:3] + copies[6:] + copies[3:6]:
        c.start()
    taps_z = kern.shape[0]
    half = (taps_z - 1) // 2
    copies[0].wait()
    lane = lax.broadcasted_iota(jnp.int32, (8, depth), 1)
    parts = [jnp.zeros((8, depth), F32) for _ in range(4)]
    for t in range(taps_z):
        parts[t % 4] = jnp.where(lane == t, kern[t], parts[t % 4])
    row = (parts[0] + parts[1]) + (parts[2] + parts[3])
    rolled = pltpu.roll(jnp.broadcast_to(row[0:1], (depth, depth)), depth - half, 1, stride=1, stride_axis=0)
    w = lax.broadcasted_iota(jnp.int32, (depth, depth), 0)
    z = lax.broadcasted_iota(jnp.int32, (depth, depth), 1)
    matrix = jnp.where(jnp.abs(z - w) <= half, rolled, 0.0)
    for c in copies[6:]:
        c.wait()
    at = 0
    for table in few:
        for t in range(table.shape[0]):
            spread[at] = jnp.full((8, depth), table[t], F32)
            at += 1
    copies[1].wait()
    copies[2].wait()
    weighted = (1.0 + 3.0 * mask[...].astype(F32)) * misfit[...]
    work[...] = lax.dot_general(
        weighted, matrix, (((1,), (1,)), ((), ())),
        precision=lax.Precision.HIGHEST, preferred_element_type=F32)
    for c in copies[3:6]:
        c.wait()
    edge[...] = states[...].astype(F32).reshape(edge.shape)
    octets = nx // 8
    for y in range(ny):
        for o in range(octets):
            own[y, pl.ds(8 * o, 8), :] = work[pl.ds(8 * o * ny + y, 8, stride=ny), :]
    width = reach + RIM

    def pack(out, right):
        start = ny - width if right else 0
        for y in range(width):
            out[y] = own[start + y]
        for k in range(RIM):
            y = ny - RIM + k if right else k
            for o in range(octets):
                out[width + k, pl.ds(8 * o, 8), :] = diffusion[pl.ds(8 * o * ny + y, 8, stride=ny), :]
        y = ny - 1 if right else 0
        for o in range(octets):
            here = pl.ds(8 * o * ny + y, 8, stride=ny)
            out[width + RIM, pl.ds(8 * o, 8), :] = labels[here, :].astype(F32)
            for s in range(steps):
                at = pl.ds((s * nx + 8 * o) * ny + y, 8, stride=ny)
                out[width + RIM + 1 + s, pl.ds(8 * o, 8), :] = edge[at, :]

    def act(right):
        pack(one, right)
        pack(two, not right)

    both_ways(right_comes_first(), act)


def own_y_kernel(reach, own, spread, part):
    ny, nx, _ = own.shape
    taps = [spread[t] for t in vectors(spread, reach)[1]]
    width = (len(taps) - 1) // 2 + RIM

    @pl.loop(0, nx // 8)
    def _(o):
        at = pl.ds(pl.multiple_of(8 * o, 8), 8)

        def write(j, value):
            part[j, at, :] = value

        blur(lambda e: own[e - width, at, :], write, taps, range(ny + 2 * RIM), range(width, width + ny))


def rest_y_kernel(reach, part, one, two, labels, diffusion, states, spread, blurred, outer, inner, left, right):
    tall, nx, depth = part.shape
    ny = tall - 2 * RIM
    taps = [spread[t] for t in vectors(spread, reach)[1]]
    width = (len(taps) - 1) // 2 + RIM

    def place(first):
        left[...] = (two if first else one)[...]
        right[...] = (one if first else two)[...]

    both_ways(right_comes_first(), place)

    for o in range(nx // 8):
        at = pl.ds(8 * o, 8)

        def read(e):
            return left[e, at, :] if e < width else right[e - width - ny, at, :]

        def write(j, value):
            blurred[pl.ds(8 * o * SLOT + JOFF - RIM + j, 8, stride=SLOT), :] = value

        blur(read, write, taps, range(tall), [*range(width), *range(width + ny, 2 * width + ny)],
             base=lambda j: part[j, at, :])

    def pack(out, upper):
        at = 0
        order = range(nx - 1, -1, -1) if upper else range(nx)
        for x in order[:width]:
            out[pl.ds(at, tall), :] = blurred[pl.ds(x * SLOT + JOFF - RIM, tall), :]
            at += tall
        for x in order[:RIM]:
            for r in range(RIM):
                out[pl.ds(at + r, 1), :] = left[width + r, pl.ds(x, 1), :]
                out[pl.ds(at + RIM + ny + r, 1), :] = right[width + r, pl.ds(x, 1), :]
            out[pl.ds(at + RIM, ny), :] = diffusion[x]
            at += tall
        x = order[0]
        out[pl.ds(at, ny), :] = labels[x].astype(F32)
        at += ny
        for s in range(states.shape[0]):
            out[pl.ds(at, ny), :] = states[s, x].astype(F32)
            at += ny

    def act(even):
        pack(inner, even)
        pack(outer, not even)

    both_ways(is_even(), act)


def rate(code, table):
    return jnp.where(code == 0, table[0], jnp.where(code == 1, table[1], table[2]))


def shares(here, there):
    inverse = 1.0 / jnp.maximum(here + there, 1e-30)
    return there * inverse, here * inverse


def inside(rows, depth):
    return lax.broadcasted_iota(jnp.int32, (rows, depth), 1) < depth - 1


def stepper(image, adj, coef, state, keep, cx, cy, cz, xl, xu, yl, yu, zl, zu, labels, bind_t, release_t, put):
    steps, ny, depth = state.shape[0], labels.shape[1], labels.shape[2]
    h, down, after = STEP_ROWS
    own_rows = slice(JOFF, JOFF + ny)
    before, next_ = slice(JOFF - 1, JOFF - 1 + ny), slice(JOFF + 1, JOFF + 1 + ny)

    def first(p, c_low, c_up, c_y, c_y_low, c_z, kept):
        a = image[p, h, :]
        total = c_up * (image[p + 1, h, :] - a) + c_low * (image[p - 1, h, :] - a)
        total += c_y * (image[p, after, :] - a) + c_y_low * (image[p, down, :] - a)
        fz = c_z * (pltpu.roll(a, depth - 1, 1) - a)
        adj[p, h, :] = kept * a + total + (fz - pltpu.roll(fz, 1, 1))

    def first_plain(p):
        first(p, cx[p - 1, h, :], cx[p, h, :], cy[p, h, :], cy[p, down, :], cz[p, h, :], keep[p, h, :])

    def second(p, c_low, s_low, state_low, c_up, s_up, state_up):
        at = own_rows
        a1, a0 = image[p, at, :], adj[p, at, :]
        s1, s0 = state[steps - 1, p, at, :], state[0, p, at, :]
        total, slopes = 0.0, 0.0

        def face(c, s, i, rows, states):
            change1, change0 = image[i, rows, :] - a1, adj[i, rows, :] - a0
            return c * change0, s * ((states[0] - s1) * change1 + (states[1] - s0) * change0)

        x = p - RIM
        for f, g in (face(c_low, s_low, p - 1, at, state_low), face(c_up, s_up, p + 1, at, state_up),
                     face(cy[p, before, :], yu[p, before, :], p, before,
                          (state[steps - 1, p, before, :], state[0, p, before, :])),
                     face(cy[p, at, :], yl[p, at, :], p, next_, (state[steps - 1, p, next_, :], state[0, p, next_, :]))):
            total, slopes = total + f, slopes + g
        nxt = functools.partial(pltpu.roll, shift=depth - 1, axis=1)
        change1, change0 = nxt(a1) - a1, nxt(a0) - a0
        both = (nxt(s1) - s1) * change1 + (nxt(s0) - s0) * change0
        fz = cz[p, at, :] * change0
        total += fz - pltpu.roll(fz, 1, 1)
        slopes += zl[p, at, :] * both + pltpu.roll(zu[p, at, :] * both, 1, 1)
        code = labels[x]
        bind, release = rate(code, bind_t), rate(code, release_t)
        b1 = 0.5 * a1 + release * (a1 - 0.5 * a1)
        put(x, -slopes, a0 + total + bind * (b1 - a0), b1 + release * (a0 - b1))

    def second_plain(p):
        at = own_rows
        second(p, cx[p - 1, at, :], xu[p - 1, at, :], (state[steps - 1, p - 1, at, :], state[0, p - 1, at, :]),
               cx[p, at, :], xl[p, at, :], (state[steps - 1, p + 1, at, :], state[0, p + 1, at, :]))

    return first, first_plain, second, second_plain


def free_slots(nx, width, even):
    return jnp.where(even, width + RIM, RIM), nx - width


def early_x_kernel(reach, blurred, inner, one, two, labels, diffusion, states, spread,
                   image, coef, state, keep, cx, cy, cz, xl, xu, yl, yu, zl, zu, done_adj, done, ext, kind, adj):
    nx, ny, depth = labels.shape
    steps = states.shape[0]
    taps_at, _, bind_at, release_at = vectors(spread, reach)
    taps = [spread[t] for t in taps_at]
    bind_t, release_t = ([spread[t, 0:1, :] for t in at] for at in (bind_at, release_at))
    width = (len(taps) - 1) // 2 + RIM
    tall = ny + 2 * RIM
    lo, own_rows = JOFF - RIM, slice(JOFF, JOFF + ny)
    outs = range(nx + 2 * RIM)

    def place(even):
        slab = inner.at[1 if even else 0]
        at = 0
        for k in range(width):
            ext[k, lo:lo + tall, :] = slab[pl.ds(at, tall), :]
            at += tall
        first, step = (nx + RIM, 1) if even else (RIM - 1, -1)
        for k in range(RIM):
            coef[first + step * k, lo:lo + tall, :] = slab[pl.ds(at, tall), :]
            at += tall
        kind[first, own_rows, :] = slab[pl.ds(at, ny), :]
        at += ny
        for s in range(steps):
            state[s, first, own_rows, :] = slab[pl.ds(at, ny), :]
            at += ny

    both_ways(is_even(), place)

    for x in range(nx):
        p = RIM + x
        coef[p, own_rows, :] = diffusion[x]
        kind[p, own_rows, :] = labels[x].astype(F32)
        for s in range(steps):
            state[s, p, own_rows, :] = states[s, x].astype(F32)

    def rims(first):
        left, right = (two, one) if first else (one, two)
        for x in range(nx):
            p, row = RIM + x, pl.ds(x, 1)
            for k in range(RIM):
                coef[p, lo + k:lo + k + 1, :] = left[width + k, row, :]
                coef[p, JOFF + ny + k:JOFF + ny + k + 1, :] = right[width + k, row, :]
            kind[p, JOFF - 1:JOFF, :] = left[width + RIM, row, :]
            kind[p, JOFF + ny:JOFF + ny + 1, :] = right[width + RIM, row, :]
            for s in range(steps):
                state[s, p, JOFF - 1:JOFF, :] = left[width + RIM + 1 + s, row, :]
                state[s, p, JOFF + ny:JOFF + ny + 1, :] = right[width + RIM + 1 + s, row, :]

    both_ways(right_comes_first(), rims)

    @pl.loop(0, SLOT // 8)
    def _(v):
        rows = pl.ds(pl.multiple_of(8 * v, 8), 8)

        def write(i, value):
            image[i, rows, :] = value

        def near(e):
            return blurred[pl.ds(pl.multiple_of((e - width) * SLOT + 8 * v, 8), 8), :]

        blur(near, write, taps, outs, range(width, width + nx))

        def add(even):
            here = range(width + nx, 2 * width + nx) if even else range(width)
            touched = outs[nx + 2 * RIM - width:] if even else outs[:width]
            blur(lambda e: ext[e - width - nx if even else width - 1 - e, rows, :], write, taps, touched, here,
                 base=lambda i: image[i, rows, :])

        both_ways(is_even(), add)

    last = inside(SLOT, depth)

    @pl.loop(0, nx + 2 * RIM - 1, unroll=9)
    def _(p):
        h = slice(0, SLOT)
        d = coef[p, h, :]
        for there, c, low, up in ((coef[p + 1, h, :], cx, xl, xu), (coef[p, 1:SLOT + 1, :], cy, yl, yu),
                                  (pltpu.roll(d, depth - 1, 1), cz, zl, zu)):
            q, r = shares(d, there)
            if c is cz:
                q, r = jnp.where(last, q, 0.0), jnp.where(last, r, 0.0)
            c[p, h, :] = 2.0 * d * q
            low[p, h, :] = 2.0 * q * q
            up[p, h, :] = 2.0 * r * r
        keep[p, h, :] = 1.0 - 0.5 * rate(kind[p, h, :], bind_t)

    even = is_even()
    lower, count = free_slots(nx, width, even)

    def put(x, *results):
        for n, value in enumerate(results):
            done[n, x + RIM - lower] = value

    _, first, _, second = stepper(image, adj, coef, state, keep, cx, cy, cz, xl, xu, yl, yu, zl, zu, labels, bind_t, release_t, put)

    @pl.loop(0, count + 2, unroll=count + 2)
    def _(n):
        first(lower - 1 + n)

    @pl.loop(0, count, unroll=count)
    def _(n):
        second(lower + n)

    def keep_nearest(even):
        for n in range(2):
            done_adj[n] = adj[width + 1 + n if even else nx + 2 * RIM - 2 - width - n]

    both_ways(even, keep_nearest)


def last_kernel(reach, part, coef, state, keep, cx, cy, cz, xl, xu, yl, yu, zl, zu, outer, labels, spread,
                done_adj, done, grad_h, adjoint_h, ext, image, adj, rim, grad, adjoint, sems):
    nx, ny, depth = labels.shape
    steps = state.shape[0]
    taps_at, _, bind_at, release_at = vectors(spread, reach)
    taps = [spread[t] for t in taps_at]
    bind_t, release_t = ([spread[t, 0:1, :] for t in at] for at in (bind_at, release_at))
    width = (len(taps) - 1) // 2 + RIM
    tall = ny + 2 * RIM
    lo, own_rows = JOFF - RIM, slice(JOFF, JOFF + ny)
    outs = range(nx + 2 * RIM)
    even = is_even()

    lower, count = free_slots(nx, width, even)
    at = pl.ds(lower - RIM, count)
    copies = [pltpu.make_async_copy(done.at[n], target, sems.at[CHUNKS + 1, n])
              for n, target in enumerate((grad_h.at[at], adjoint_h.at[0, at], adjoint_h.at[1, at]))]
    for c in copies:
        c.start()

    for k in range(width):
        ext[k, lo:lo + tall, :] = outer[pl.ds(k * tall, tall), :]
    for k in range(RIM):
        rim[k, lo:lo + tall, :] = outer[pl.ds((width + k) * tall, tall), :]
    tail = (width + RIM) * tall
    rim[RIM, own_rows, :] = outer[pl.ds(tail, ny), :]
    for s in range(steps):
        rim[RIM + 1 + s, own_rows, :] = outer[pl.ds(tail + (1 + s) * ny, ny), :]

    @pl.loop(0, SLOT // 8)
    def _(v):
        rows = pl.ds(pl.multiple_of(8 * v, 8), 8)

        def write(i, value):
            image[i, rows, :] = value

        def add(even):
            far = range(width) if even else range(width + nx, 2 * width + nx)
            touched = outs[:width] if even else outs[nx + 2 * RIM - width:]
            blur(lambda e: ext[width - 1 - e if even else e - width - nx, rows, :], write, taps, touched, far,
                 base=lambda i: part[i, rows, :])
            for i in outs:
                if i not in touched and min(abs(i - k) for k in touched) <= 3:
                    image[i, rows, :] = part[i, rows, :]

        both_ways(even, add)

    def put(x, *results):
        grad[x], adjoint[0, x], adjoint[1, x] = results

    first, first_plain, second, second_plain = stepper(
        image, adj, coef, state, keep, cx, cy, cz, xl, xu, yl, yu, zl, zu, labels, bind_t, release_t, put)
    h, down, after = STEP_ROWS

    def coupling(here, there):
        q, _ = shares(here, there)
        return 2.0 * here * q

    def send(n, x, count):
        at = pl.ds(x, count)
        pairs = ((grad.at[at], grad_h.at[at]), (adjoint.at[0, at], adjoint_h.at[0, at]),
                 (adjoint.at[1, at], adjoint_h.at[1, at]))
        return [pltpu.make_async_copy(a, b, sems.at[n, m]) for m, (a, b) in enumerate(pairs)]

    def near_rim(even):
        near, far, tile = (1, 0, RIM) if even else (nx + RIM, nx + RIM + 1, nx + RIM - 1)
        d, d_far, d_tile = rim[0, h, :], rim[1, h, :], coef[tile, h, :]
        c_tile, c_far = coupling(d, d_tile), coupling(d, d_far)
        c_z = jnp.where(inside(SLOT, depth), coupling(d, pltpu.roll(d, depth - 1, 1)), 0.0)
        kept = 1.0 - 0.5 * rate(rim[RIM, h, :], bind_t)
        c_low, c_up = (c_far, c_tile) if even else (c_tile, c_far)
        first(near, c_low, c_up, coupling(d, rim[0, after, :]), coupling(d, rim[0, down, :]), c_z, kept)
        inner_face = cx[tile, h, :] if even else cx[tile - 1, h, :]
        c_low, c_up = (c_tile, inner_face) if even else (inner_face, c_tile)
        first(tile, c_low, c_up, cy[tile, h, :], cy[tile, down, :], cz[tile, h, :], keep[tile, h, :])

    def near_rim_second(even):
        tile = RIM if even else nx + RIM - 1
        at = own_rows
        q, r = shares(coef[tile, at, :], rim[0, at, :])
        far = (2.0 * coef[tile, at, :] * q, 2.0 * q * q, (rim[RIM + steps, at, :], rim[RIM + 1, at, :]))
        if even:
            second(tile, *far, cx[tile, at, :], xl[tile, at, :],
                   (state[steps - 1, tile + 1, at, :], state[0, tile + 1, at, :]))
        else:
            second(tile, cx[tile - 1, at, :], xu[tile - 1, at, :],
                   (state[steps - 1, tile - 1, at, :], state[0, tile - 1, at, :]), *far)

    both_ways(even, near_rim)

    def take(even):
        for n in range(2):
            adj[width + 1 + n if even else nx + 2 * RIM - 2 - width - n] = done_adj[n]

    both_ways(even, take)
    left = width - RIM
    low = jnp.where(even, RIM + 1, nx + 1 - left)

    @pl.loop(0, left, unroll=left)
    def _(n):
        first_plain(low + n)

    both_ways(even, near_rim_second)
    more = send(0, jnp.where(even, 0, nx - 1), 1)
    for c in more:
        c.start()
    copies += more
    base = jnp.where(even, RIM + 1, nx - left)
    size = (left + 1) // CHUNKS

    @pl.loop(0, CHUNKS)
    def _(n):
        for k in range(size):
            second_plain(base + n * size + k)
        for c in send(n + 1, base - RIM + n * size, size):
            c.start()

    for n in range(CHUNKS):
        copies += send(n + 1, base - RIM + n * size, size)
    for c in copies:
        c.wait()


def swap_along_gy(shape, parity):
    nx, ny = shape
    pairs = []
    for i in range(nx):
        for j in range((parity + i + i // 2 + 1) % 2, ny - 1, 2):
            a, b = i * ny + j, i * ny + j + 1
            pairs += [(a, b), (b, a)]
    return pairs


def shards(misfit, bleach_mask, labels, diffusion, bind_table, release_table, kern_x, kern_y, kern_z, free_states):
    nx, ny, depth = misfit.shape
    steps = free_states.shape[0]
    reach = (kern_x.shape[0] - 1) // 2
    width = reach + RIM
    tall = ny + 2 * RIM
    shape = (lax.axis_size("gx"), lax.axis_size("gy"))
    vmem = pl.BlockSpec(memory_space=pltpu.VMEM)
    hbm = pl.BlockSpec(memory_space=pl.ANY)
    params = pltpu.CompilerParams(vmem_limit_bytes=24 * 1024 * 1024)
    flat = (nx * ny, depth)
    array = jax.ShapeDtypeStruct

    def in_hbm(x):
        return pltpu.with_memory_space_constraint(x, pltpu.MemorySpace.HBM)

    slots = width + RIM + 1 + steps
    slab = array((slots, nx, depth), F32)
    few = (kern_x, kern_y, bind_table, release_table)
    own, one, two, spread, held_labels, held_diffusion, held_states = pl.pallas_call(
        functools.partial(first_kernel, reach),
        out_shape=[array((ny, nx, depth), F32), slab, slab, array((sum(t.shape[0] for t in few), 8, depth), F32),
                   array(flat, jnp.int32), array(flat, F32), array(free_states.shape, free_states.dtype)],
        in_specs=[hbm] * (6 + len(few)),
        out_specs=[vmem] * 7,
        scratch_shapes=[
            pltpu.VMEM(flat, F32), pltpu.VMEM(flat, jnp.int32), pltpu.SMEM(kern_z.shape, F32),
            pltpu.VMEM(flat, F32), pltpu.VMEM((steps * nx * ny, depth), F32),
            *(pltpu.SMEM(t.shape, F32) for t in few), pltpu.SemaphoreType.DMA((6 + len(few),))],
        compiler_params=params,
        name="weigh_blur_z",
    )(in_hbm(misfit.reshape(flat)), in_hbm(bleach_mask.reshape(flat)), in_hbm(labels.reshape(flat)),
      in_hbm(diffusion.reshape(flat)), in_hbm(free_states), in_hbm(kern_z), *map(in_hbm, few))
    labels, diffusion = held_labels.reshape(labels.shape), held_diffusion.reshape(diffusion.shape)
    one = lax.ppermute(one, AXES, swap_along_gy(shape, 0))
    two = lax.ppermute(two, AXES, swap_along_gy(shape, 1))

    part = pl.pallas_call(
        functools.partial(own_y_kernel, reach),
        out_shape=array((tall, nx, depth), F32),
        in_specs=[vmem] * 2,
        out_specs=vmem,
        compiler_params=params,
        cost_estimate=pl.CostEstimate(flops=4_000_000, bytes_accessed=700_000, transcendentals=0),
        name="own_y",
    )(own, spread)

    rows = (width + RIM) * tall + (1 + steps) * ny
    slab = array((rows, depth), F32)
    blurred, outer, inner = pl.pallas_call(
        functools.partial(rest_y_kernel, reach),
        out_shape=[array((nx * SLOT, depth), F32), slab, slab],
        in_specs=[vmem] * 7,
        out_specs=[vmem] * 3,
        scratch_shapes=[pltpu.VMEM((slots, nx, depth), F32)] * 2,
        compiler_params=params,
        name="rest_y",
    )(part, one, two, labels, diffusion, held_states, spread)

    line = shape[1]
    across = []
    for i in range(1, shape[0] - 1, 2):
        for j in range(line):
            a, b = i * line + j, (i + 1) * line + j
            across += [(a, b), (b, a)]
    within = [[i * line + j, (i + 1) * line + j] for i in range(0, shape[0], 2) for j in range(line)]
    outer = lax.ppermute(outer, AXES, across)
    inner = lax.all_gather(inner, AXES, axis_index_groups=within)

    around = (nx + 2 * RIM, HIGH, depth)
    field = array(around, F32)
    *early, done_adj, done = pl.pallas_call(
        functools.partial(early_x_kernel, reach),
        out_shape=[field, field, array((steps, *around), F32)] + [field] * 10
        + [array((2, *around[1:]), F32), array((3, nx - width, ny, depth), F32)],
        in_specs=[vmem] * 8,
        out_specs=[vmem] * 15,
        scratch_shapes=[pltpu.VMEM((width, SLOT, depth), F32), pltpu.VMEM(around, F32), pltpu.VMEM(around, F32)],
        compiler_params=params,
        cost_estimate=pl.CostEstimate(flops=8_000_000, bytes_accessed=3_000_000, transcendentals=0),
        name="early_x",
    )(blurred, inner, one, two, labels, diffusion, held_states, spread)

    tile = (nx, ny, depth)
    grad, adjoint = pl.pallas_call(
        functools.partial(last_kernel, reach),
        out_shape=[array(tile, F32), array((2, *tile), F32)],
        in_specs=[vmem] * 18,
        out_specs=[hbm] * 2,
        scratch_shapes=[
            pltpu.VMEM((width, SLOT, depth), F32),
            pltpu.VMEM(around, F32),
            pltpu.VMEM(around, F32),
            pltpu.VMEM((RIM + 1 + steps, HIGH, depth), F32),
            pltpu.VMEM(tile, F32),
            pltpu.VMEM((2, *tile), F32),
            pltpu.SemaphoreType.DMA((CHUNKS + 2, 3)),
        ],
        compiler_params=params,
        name="late_x_steps",
    )(*early, outer, labels, spread, done_adj, done)
    return grad, adjoint


def solution(mesh):
    tile = P("gx", "gy", None)
    in_specs = (tile, tile, tile, tile, P(), P(), P(), P(), P(), P(None, "gx", "gy", None))
    out_specs = (tile, P(None, "gx", "gy", None))
    return jax.shard_map(shards, mesh=mesh, in_specs=in_specs, out_specs=out_specs, check_vma=False)
```
